32 devices in a mesh: groups: 1, slab: 8 (over z, y), temp: 2 (over x), pen: 2 (over core).
Axes of the slice: x: 2, y: 2, z: 4, core: 2. Of those that a mesh axis runs over, the one named last changes fastest.
Arguments:
- moments: float32 [2, 3, 128, 128, 128], P(('groups', 'temp'), None, ('slab', 'pen')), may hold values from -1 to 1, as said below
- couplings: bfloat16 [3, 128, 128, 128], P('groups', ('slab', 'pen')), may hold values from -6 to 6
- noise: bfloat16 [2, 2, 3, 128, 128, 128], P(None, ('groups', 'temp'), None, ('slab', 'pen')), may hold values from -6 to 6
- kernel: float32 [6, 128, 128, 128], P(None, None, ('slab', 'pen')), may hold values from -2.5 to 2.5, as said below
- temps: float32 [2], replicated, may hold values from 0.05 to 2
- order: int32 [2], P('groups'), may hold values from 0 to 1, each once
- accept: int32 [2], P('groups'), may hold values 0 or 1
Outputs:
- moments_out: float32 [2, 3, 128, 128, 128], P(('groups', 'temp'), None, ('slab', 'pen'))
- labels: int32 [2], P('groups')
The draws below stay inside these ranges and needn't reach their ends.
Inputs may be any that keep to these rules, and one draw needn't show every extreme that they name: `moments`: every moment vector (the three entries of one replica at one cell) has length one up to float32 rounding. kernel[c, i, j, l] equals kernel[c, (128 - i) % 128, (128 - j) % 128, (128 - l) % 128]. `order`: each temperature index appears once.
All inputs are finite; a program needn't handle non-finite values.
Results may differ from the reference program's by a relative error of at most 0.0003.
Values sent between devices are 32-bit elements; how exact they have to be, the bound alone decides.
No kernel may reach another device: no remote copies, remote signals or barrier semaphores. Data moves between devices by JAX's collectives and lax.ppermute only.
A program may use at most 128 MiB of HBM per device.

```python
import math
import jax
import jax.numpy as jnp
from jax import lax

GRID = 128
STEPS = 2
REPL = 2


def draw_moments(key, part):
    shape = (REPL, GRID, GRID, GRID)
    key_height, key_phase = jax.random.split(jax.random.fold_in(key, 11))
    height = jax.random.uniform(key_height, shape, jnp.float32, -1.0, 1.0)
    phase = jax.random.uniform(key_phase, shape, jnp.float32, 0.0, 2.0 * math.pi)
    radial = jnp.sqrt(jnp.maximum(1.0 - height * height, 0.0))
    return jnp.stack([radial * jnp.cos(phase), radial * jnp.sin(phase), height], axis=1).astype(jnp.float32)


def draw_kernel(key, part):
    positions = jnp.arange(GRID, dtype=jnp.float32)
    wave = jnp.sin(2.0 * math.pi * positions / GRID)
    wave_x = wave[:, None, None]
    wave_y = wave[None, :, None]
    wave_z = wave[None, None, :]
    denominator = wave_x * wave_x + wave_y * wave_y + wave_z * wave_z + 0.05
    combos = [(wave_x, wave_x), (wave_y, wave_y), (wave_z, wave_z), (wave_x, wave_y), (wave_x, wave_z), (wave_y, wave_z)]
    physical = jnp.stack([left_wave * right_wave / denominator for left_wave, right_wave in combos])
    rough_key = jax.random.fold_in(key, 23)
    rough = jnp.clip(jax.random.normal(rough_key, (6, GRID, GRID, GRID), jnp.float32), -3.0, 3.0) * 0.4
    mirrored = jnp.roll(jnp.flip(rough, (1, 2, 3)), 1, axis=(1, 2, 3))
    return (0.8 * physical + 0.5 * (rough + mirrored)).astype(jnp.float32)


def plant(entries, key, least, top_value):
    longest = entries.shape.index(max(entries.shape))
    spots = []
    for shift in (0, 1):
        where = [jax.random.randint(jax.random.fold_in(key, axis), (), 0, length) for axis, length in enumerate(entries.shape)]
        where[longest] = (where[longest] + shift) % entries.shape[longest]
        spots.append(tuple(where))
    return entries.at[spots[0]].set(least).at[spots[1]].set(top_value)


def block_levels(rng, extent, cuts, low, high):
    factor_of, own = 1.0, jax.random.fold_in(rng, 6)
    for dim, blocks in cuts:
        draws = jnp.exp(jax.random.uniform(jax.random.fold_in(own, dim), (blocks,), jnp.float32, low / len(cuts), high / len(cuts)))
        factor_of = factor_of * jnp.repeat(draws, extent[dim] // blocks).reshape([-1 if axis == dim else 1 for axis in range(len(extent))])
    return factor_of


def scatter_about(rng, extent, width, most, pieces=(), held_as=jnp.bfloat16):
    factor_of = block_levels(rng, extent, pieces, -0.22, 0.18) if pieces else 1.0
    entries = jax.random.normal(rng, extent, jnp.float32) * width * factor_of
    return jnp.minimum(jnp.maximum(entries, -most), most).astype(held_as)


def setup_inputs(seed: int = 0, part: int = 0) -> dict:
    key_list = jax.random.split(jax.random.key(seed), 8)
    own_keys = jax.random.split(jax.random.fold_in(key_list[7], part), 8)
    moments = draw_moments(jax.random.fold_in(jax.random.fold_in(key_list[7], part), 71), part)
    couplings = scatter_about(own_keys[1], (3, GRID, GRID, GRID), 1.0, 6.0, ((1, 16),))
    noise = scatter_about(own_keys[2], (STEPS, REPL, 3, GRID, GRID, GRID), 1.0, 6.0, ((1, 2), (3, 16)))
    kernel = draw_kernel(jax.random.fold_in(key_list[7], 71), part)
    temps = jnp.clip(jnp.exp(jax.random.uniform(key_list[4], (REPL,), jnp.float32, math.log(0.05), math.log(2.0))), 0.05, 2.0)
    order = jax.random.permutation(own_keys[5], REPL).astype(jnp.int32)
    accept = plant((jax.random.randint(own_keys[6], (REPL,), 0, 4) < 3).astype(jnp.int32), jax.random.fold_in(own_keys[6], 1), 0, 1)
    return {"moments": moments, "couplings": couplings, "noise": noise, "kernel": kernel, "temps": temps, "order": order, "accept": accept}


TIME_STEP = 0.1
DAMPING = 0.5

def cross(left, right, axis):
    left_parts = [lax.index_in_dim(left, component, axis, keepdims=False) for component in range(3)]
    right_parts = [lax.index_in_dim(right, component, axis, keepdims=False) for component in range(3)]
    result = [left_parts[1] * right_parts[2] - left_parts[2] * right_parts[1], left_parts[2] * right_parts[0] - left_parts[0] * right_parts[2], left_parts[0] * right_parts[1] - left_parts[1] * right_parts[0]]
    return jnp.stack(result, axis=axis)

def pair_labels(order, accept):
    slot_index = jnp.arange(order.shape[0], dtype=jnp.int32)
    position = lax.optimization_barrier(jnp.sum(jnp.where(order[None, :] == slot_index[:, None], slot_index[None, :], 0), axis=1)).astype(jnp.int32)
    mate_position = position + 1 - 2 * (position % 2)
    partner = lax.optimization_barrier(jnp.sum(jnp.where(slot_index[None, :] == mate_position[:, None], order[None, :], 0), axis=1)).astype(jnp.int32)
    partner_flag = lax.optimization_barrier(jnp.sum(jnp.where(slot_index[None, :] == partner[:, None], accept[None, :], 0), axis=1)).astype(jnp.int32)
    accepted = accept * partner_flag
    return jnp.where(accepted == 1, partner, slot_index).astype(jnp.int32)

def slot_sigma(labels, temps):
    slot_index = jnp.arange(temps.shape[0], dtype=jnp.int32)
    picked = lax.optimization_barrier(jnp.sum(jnp.where(labels[:, None] == slot_index[None, :], temps[None, :], jnp.zeros_like(temps)[None, :]), axis=1))
    return jnp.sqrt(2.0 * DAMPING * picked / TIME_STEP)

def neighbor_sum(moment_field, bond_field):
    summed = jnp.zeros_like(moment_field)
    for grid_axis in range(3):
        coupling = bond_field[grid_axis]
        summed = summed + coupling * jnp.roll(moment_field, -1, grid_axis + 1) + jnp.roll(coupling * moment_field, 1, grid_axis + 1)
    return summed

def dipole(moment_field, kernel):
    spectrum = jnp.fft.fftn(moment_field, axes=(1, 2, 3))
    parts = [spectrum[0], spectrum[1], spectrum[2]]
    fields = [-(kernel[0] * parts[0] + kernel[3] * parts[1] + kernel[4] * parts[2]), -(kernel[3] * parts[0] + kernel[1] * parts[1] + kernel[5] * parts[2]), -(kernel[4] * parts[0] + kernel[5] * parts[1] + kernel[2] * parts[2])]
    return jnp.real(jnp.fft.ifftn(jnp.stack(fields), axes=(1, 2, 3)))

def advance(moment_field, local_field, noise_scale, noise_step):
    effective = local_field + noise_scale * noise_step.astype(jnp.float32)
    torque = cross(moment_field, effective, 0)
    stepped = moment_field - TIME_STEP * (torque + DAMPING * cross(moment_field, torque, 0))
    return stepped * lax.rsqrt(lax.optimization_barrier(jnp.sum(stepped * stepped, axis=0, keepdims=True)))

def reference(moments, couplings, noise, kernel, temps, order, accept):
    labels = pair_labels(order, accept)
    slot_index = jnp.arange(temps.shape[0], dtype=jnp.int32)
    first_scale = slot_sigma(slot_index, temps)
    second_scale = slot_sigma(labels, temps)
    bond_field = couplings.astype(jnp.float32)

    def one_replica(packed):
        moment_field, noises, scale_one, scale_two = packed
        for step_index, noise_scale in ((0, scale_one), (1, scale_two)):
            local_field = neighbor_sum(moment_field, bond_field) + dipole(moment_field, kernel)
            moment_field = advance(moment_field, local_field, noise_scale, noises[step_index])
        return moment_field
    moved = lax.map(one_replica, (moments, jnp.moveaxis(noise, 1, 0), first_scale, second_scale))
    return (moved, labels)
```

```python
import functools
import math

import jax
import jax.numpy as jnp
from jax import lax
from jax.experimental import pallas as pl
from jax.experimental.pallas import tpu as pltpu
from jax.sharding import PartitionSpec as P

TIME_STEP = 0.1
DAMPING = 0.5
AXES = ("slab", "pen")
CHUNKS = 2
VMEM_BYTES = 40 * 1024 * 1024


def shifted(block, axis, distance):
    devices = range(lax.axis_size(axis))
    route = [((i - distance) % len(devices), i) for i in devices]
    return lax.ppermute(block, axis, route)


def cross(left, right, axis):
    left_parts = [lax.index_in_dim(left, component, axis, keepdims=False) for component in range(3)]
    right_parts = [
        lax.index_in_dim(right, component, axis, keepdims=False) for component in range(3)
    ]
    result = [
        left_parts[1] * right_parts[2] - left_parts[2] * right_parts[1],
        left_parts[2] * right_parts[0] - left_parts[0] * right_parts[2],
        left_parts[0] * right_parts[1] - left_parts[1] * right_parts[0],
    ]
    return jnp.stack(result, axis=axis)


def pair_labels(order, accept):
    slot_index = jnp.arange(order.shape[0], dtype=jnp.int32)
    position = jnp.sum(
        jnp.where(order[None, :] == slot_index[:, None], slot_index[None, :], 0), axis=1
    )
    mate_position = position + 1 - 2 * (position % 2)
    partner = jnp.sum(
        jnp.where(slot_index[None, :] == mate_position[:, None], order[None, :], 0), axis=1
    )
    partner_flag = jnp.sum(
        jnp.where(slot_index[None, :] == partner[:, None], accept[None, :], 0), axis=1
    )
    accepted = accept * partner_flag
    return jnp.where(accepted == 1, partner, slot_index)


def slot_sigma(labels, temps):
    slot_index = jnp.arange(temps.shape[0], dtype=jnp.int32)
    picked = jnp.sum(
        jnp.where(
            labels[:, None] == slot_index[None, :], temps[None, :], jnp.zeros_like(temps)[None, :]
        ),
        axis=1,
    )
    return jnp.sqrt(2.0 * DAMPING * picked / TIME_STEP)


def angle_tables(length):
    positions = jnp.arange(length, dtype=jnp.int32)
    product = positions[:, None] * positions[None, :] % length
    angles = 2.0 * math.pi / length * product.astype(jnp.float32)
    return (jnp.cos(angles), jnp.sin(angles))


def twist(packed, cosine_table, sine_table, pattern, orientation):
    cosine_part = jnp.einsum(pattern, packed, cosine_table, precision=lax.Precision.HIGHEST)
    sine_part = jnp.einsum(pattern, packed, sine_table, precision=lax.Precision.HIGHEST)
    middle = packed.shape[-1] // 2
    turned = jnp.concatenate([sine_part[..., middle:], -sine_part[..., :middle]], axis=-1)
    return cosine_part + orientation * turned


def pair_twist(stacked, cosine_table, sine_table, pattern, orientation):
    real_part = stacked[:, 0]
    imag_part = stacked[:, 1]
    real_cos = jnp.einsum(pattern, real_part, cosine_table, precision=lax.Precision.HIGHEST)
    real_sin = jnp.einsum(pattern, real_part, sine_table, precision=lax.Precision.HIGHEST)
    imag_cos = jnp.einsum(pattern, imag_part, cosine_table, precision=lax.Precision.HIGHEST)
    imag_sin = jnp.einsum(pattern, imag_part, sine_table, precision=lax.Precision.HIGHEST)
    return jnp.stack([real_cos + orientation * imag_sin, imag_cos - orientation * real_sin], axis=1)


def apply_kernel(spectrum, widened, replicas):
    shaped = spectrum.reshape((replicas, 3) + spectrum.shape[1:])
    comp_one, comp_two, comp_three = (shaped[:, 0], shaped[:, 1], shaped[:, 2])
    result = [
        -(widened[0] * comp_one + widened[3] * comp_two + widened[4] * comp_three),
        -(widened[3] * comp_one + widened[1] * comp_two + widened[5] * comp_three),
        -(widened[4] * comp_one + widened[5] * comp_two + widened[2] * comp_three),
    ]
    return jnp.stack(result, axis=1).reshape(spectrum.shape)


def advance(moment_field, local_field, noise_scale, noise_step):
    effective = local_field + noise_scale[:, None, None, None, None] * noise_step.astype(
        jnp.float32
    )
    torque = cross(moment_field, effective, 1)
    stepped = moment_field - TIME_STEP * (torque + DAMPING * cross(moment_field, torque, 1))
    return stepped * lax.rsqrt(jnp.sum(stepped * stepped, axis=1, keepdims=True))


def neighbor_sum(moment_field, bond_field):
    coupling_first = bond_field[0]
    carried = coupling_first * moment_field
    above = shifted(moment_field[:, :, :1], ("slab", "pen"), -1)
    below = shifted(carried[:, :, -1:], ("slab", "pen"), 1)
    upward = jnp.concatenate([moment_field[:, :, 1:], above], axis=2)
    downward = jnp.concatenate([below, carried[:, :, :-1]], axis=2)
    summed = coupling_first * upward + downward
    for grid_axis in (1, 2):
        coupling = bond_field[grid_axis]
        summed = (
            summed
            + coupling * jnp.roll(moment_field, -1, grid_axis + 2)
            + jnp.roll(coupling * moment_field, 1, grid_axis + 2)
        )
    return summed


def plain_on_device(moments, couplings, noise, kernel, temps, order, accept):
    replicas = moments.shape[0]
    planes = moments.shape[2]
    grid_width = moments.shape[3]
    grid_depth = moments.shape[4]
    slab_count = lax.axis_size("slab")
    pen_count = lax.axis_size("pen")
    slices = slab_count * pen_count
    row_block = grid_width // slices
    channels = 3 * replicas
    low_count = grid_depth // 2
    cosine_depth, sine_depth = angle_tables(grid_depth)
    cosine_width, sine_width = angle_tables(grid_width)
    inverse_cosine = cosine_width / grid_width
    inverse_sine = sine_width / grid_width
    low_weights = jnp.where(jnp.arange(low_count) == 0, 1.0, 2.0).astype(jnp.float32)
    forward_lower = jnp.concatenate(
        [cosine_depth[:, :low_count], -sine_depth[:, :low_count]], axis=1
    )
    backward_lower = (
        jnp.concatenate(
            [
                low_weights[:, None] * cosine_depth[:low_count],
                -low_weights[:, None] * sine_depth[:low_count],
            ],
            axis=0,
        )
        / grid_depth
    )
    kernel_lower = jnp.concatenate([kernel[..., :low_count], kernel[..., :low_count]], axis=-1)
    edge_column = cosine_depth[:, low_count]
    edge_row = cosine_depth[low_count] / grid_depth
    edge_kernel = jnp.swapaxes(kernel[..., low_count], 1, 2)[:, None]
    bond_field = couplings.astype(jnp.float32)
    labels = pair_labels(order, accept)
    slot_index = jnp.arange(temps.shape[0], dtype=jnp.int32)
    offset = lax.axis_index("temp") * replicas
    own_slots = lax.dynamic_slice_in_dim(slot_index, offset, replicas)
    own_labels = lax.dynamic_slice_in_dim(labels, offset, replicas)
    scales = (slot_sigma(own_slots, temps), slot_sigma(own_labels, temps))
    moment_field = moments
    for step_index in range(2):
        flattened = moment_field.reshape(channels, planes, grid_width, grid_depth)
        dipole_lower_part = jnp.dot(flattened, forward_lower, precision=lax.Precision.HIGHEST)
        dipole_lower_part = twist(dipole_lower_part, cosine_width, sine_width, "cxyw,yk->cxkw", 1.0)
        edge = jnp.dot(flattened, edge_column, precision=lax.Precision.HIGHEST)
        edge_real = jnp.einsum("cxy,yk->ckx", edge, cosine_width, precision=lax.Precision.HIGHEST)
        edge_imag = -jnp.einsum("cxy,yk->ckx", edge, sine_width, precision=lax.Precision.HIGHEST)
        edge_edge_in = jnp.stack([edge_real, edge_imag], axis=1).reshape(
            channels, 2, slices, row_block, 1, planes
        )
        edge_edge_moved = lax.all_to_all(
            edge_edge_in, ("slab", "pen"), split_axis=2, concat_axis=4, tiled=True
        )
        dipole_edge_pair = edge_edge_moved.reshape(channels, 2, row_block, grid_width)
        lower_lower_in = dipole_lower_part.reshape(
            channels, 1, planes, slices, row_block, dipole_lower_part.shape[-1]
        )
        lower_lower_out = lax.all_to_all(
            lower_lower_in, ("slab", "pen"), split_axis=3, concat_axis=1, tiled=True
        )
        dipole_lower_part = lower_lower_out.reshape(
            channels, grid_width, row_block, dipole_lower_part.shape[-1]
        )
        dipole_edge_pair = pair_twist(
            dipole_edge_pair, cosine_width, sine_width, "cyx,xk->cyk", 1.0
        )
        dipole_edge_pair = apply_kernel(dipole_edge_pair, edge_kernel, replicas)
        dipole_edge_pair = pair_twist(
            dipole_edge_pair, inverse_cosine, inverse_sine, "cyx,xk->cyk", -1.0
        )
        dipole_lower_part = twist(dipole_lower_part, cosine_width, sine_width, "cxyw,xk->ckyw", 1.0)
        dipole_lower_part = apply_kernel(dipole_lower_part, kernel_lower, replicas)
        dipole_lower_part = twist(
            dipole_lower_part, inverse_cosine, inverse_sine, "cxyw,xk->ckyw", -1.0
        )
        edge_in = dipole_edge_pair.reshape(channels, 2, 1, row_block, slices, planes)
        edge_moved = lax.all_to_all(
            edge_in, ("slab", "pen"), split_axis=4, concat_axis=2, tiled=True
        )
        dipole_edge_pair = edge_moved.reshape(channels, 2, grid_width, planes)
        lower_in = dipole_lower_part.reshape(
            channels, slices, planes, 1, row_block, dipole_lower_part.shape[-1]
        )
        lower_out = lax.all_to_all(
            lower_in, ("slab", "pen"), split_axis=1, concat_axis=3, tiled=True
        )
        dipole_lower_part = lower_out.reshape(
            channels, planes, grid_width, dipole_lower_part.shape[-1]
        )
        dipole_lower_part = twist(
            dipole_lower_part, inverse_cosine, inverse_sine, "cxyw,yk->cxkw", -1.0
        )
        edge_field = jnp.einsum(
            "ckx,ky->cxy", dipole_edge_pair[:, 0], inverse_cosine, precision=lax.Precision.HIGHEST
        ) - jnp.einsum(
            "ckx,ky->cxy", dipole_edge_pair[:, 1], inverse_sine, precision=lax.Precision.HIGHEST
        )
        summed = (
            jnp.dot(dipole_lower_part, backward_lower, precision=lax.Precision.HIGHEST)
            + edge_field[..., None] * edge_row
        )
        local_field = neighbor_sum(moment_field, bond_field) + summed.reshape(moment_field.shape)
        moment_field = advance(moment_field, local_field, scales[step_index], noise[step_index])
    return (moment_field, labels)


def split(value):
    high = value.astype(jnp.bfloat16)
    low = (value - high.astype(jnp.float32)).astype(jnp.bfloat16)
    return high, low


def stacked_parts(value):
    high, low = split(value)
    return jnp.concatenate([high, high, low], axis=0)


def product(left, right):
    return jnp.dot(left, right, preferred_element_type=jnp.float32)


def table_parts(table):
    high = lax.reduce_precision(table, 8, 7)
    return jnp.concatenate([high, lax.reduce_precision(table - high, 8, 7), high], axis=1).astype(
        jnp.bfloat16
    )


def turn(value):
    return pltpu.roll(value, value.shape[-1] // 2, value.ndim - 1)


def lane_index(shape):
    return lax.broadcasted_iota(jnp.int32, shape, len(shape) - 1)


def forward_kernel(field_ref, depth_ref, table_ref, mask_ref, *out_refs):
    _, planes, width, depth = field_ref.shape
    half = depth // 2
    lane = lane_index((width, depth))
    signs = jnp.where(lane == 0, 0.0, jnp.where(lane < half, 1.0, -1.0))
    own = mask_ref[0]
    other = mask_ref[1] > 0.5
    part = table_ref.shape[0] // len(out_refs)
    for component in range(3):
        high, low = split(field_ref[component].reshape(planes * width, depth))
        lines = product(jnp.concatenate([high, high, low], axis=1), depth_ref[...])
        extra = jnp.zeros((width, depth), jnp.float32)
        columns = []
        for plane in range(planes):
            line = lines[plane * width : (plane + 1) * width]
            turned = turn(line)
            moved = pltpu.roll(turned, plane, 1) if plane else turned
            extra = jnp.where(lane == plane, moved, extra)
            columns.append(stacked_parts(jnp.concatenate([line, turned * signs], axis=0)))
        columns.append(stacked_parts(jnp.concatenate([extra, -turn(extra)], axis=0)))
        mixed = product(table_ref[...], jnp.concatenate(columns, axis=1))
        extra = mixed[:, planes * depth :]
        for plane in range(planes):
            value = mixed[:, plane * depth : (plane + 1) * depth]
            value = value - own * pltpu.roll(extra, half - plane, 1)
            back = pltpu.roll(extra, depth - plane, 1) if plane else extra
            value = jnp.where(other, back, value)
            for index, out_ref in enumerate(out_refs):
                out_ref[component, pl.ds(plane, part, stride=planes), :] = value[
                    index * part : (index + 1) * part
                ]


def middle_kernel(start, inner, kernel_ref, weight_ref, table_ref, inverse_ref, *refs):
    in_refs, out_refs = refs[:inner], refs[inner:]
    outer, _, rows, planes, depth = in_refs[0].shape
    half = depth // 2
    count = inner * outer * planes
    row_block = kernel_ref.shape[1] // count
    lane = lane_index((count, depth))
    signs = jnp.where(lane < half, 1.0, -1.0)
    order = ((0, 3, 4), (3, 1, 5), (4, 5, 2))
    weights = [weight_ref[i : i + 1, :] for i in range(6)]
    for row in range(rows):
        spectrum, columns = [], []
        edge = start + row == 0
        for component in range(3):
            block = jnp.concatenate(
                [ref[:, component, row].reshape(outer * planes, depth) for ref in in_refs], axis=0
            )
            turned = turn(block)
            columns.append(stacked_parts(jnp.concatenate([block, turned * signs], axis=0)))
            if edge:
                mirror = jnp.concatenate([block * signs, -turned], axis=0)
                spectrum.append(stacked_parts(mirror))
        mixed = product(table_ref[...], jnp.concatenate(columns + spectrum, axis=1))
        spectrum = [mixed[:, i * depth : (i + 1) * depth] for i in range(mixed.shape[1] // depth)]
        totals = [None] * 3
        for entry in range(6):
            raw = kernel_ref[entry, pl.ds(start + row, count, stride=row_block), :]
            raw_turned = turn(raw)
            pick = 2 if edge else 0
            value = raw * weights[pick] + raw_turned * weights[pick + 1]
            for i in range(3):
                for j in range(3):
                    if order[i][j] == entry:
                        term = value * spectrum[j]
                        totals[i] = term if totals[i] is None else totals[i] + term
            if edge:
                value = raw * weights[4] + raw_turned * weights[5]
                for i in range(3):
                    for j in range(3):
                        if order[i][j] == entry:
                            totals[i] = totals[i] + value * spectrum[3 + j]
        columns = [
            stacked_parts(jnp.concatenate([total, turn(total) * signs], axis=0)) for total in totals
        ]
        mixed = product(inverse_ref[...], jnp.concatenate(columns, axis=1))
        for component in range(3):
            value = mixed[:, component * depth : (component + 1) * depth]
            for index, out_ref in enumerate(out_refs):
                size = outer * planes
                out_ref[:, component, row] = value[index * size : (index + 1) * size].reshape(
                    outer, planes, depth
                )


def gathered_columns(component, in_refs, mask_ref, table_ref, planes):
    part = in_refs[0].shape[1] // planes
    columns = []
    for plane in range(planes):
        value = jnp.concatenate(
            [ref[component, pl.ds(plane, part, stride=planes), :] for ref in in_refs], axis=0
        )
        turned = turn(value)
        top = value * mask_ref[0] + turned * mask_ref[1]
        bottom = value * mask_ref[2] + turned * mask_ref[3]
        columns.append(stacked_parts(jnp.concatenate([top, bottom], axis=0)))
    return product(table_ref[...], jnp.concatenate(columns, axis=1))


def backward_kernel(table_ref, mask_ref, *refs):
    in_refs, out_ref = refs[:-1], refs[-1]
    _, planes, _, depth = out_ref.shape
    for component in range(3):
        mixed = gathered_columns(component, in_refs, mask_ref, table_ref, planes)
        for plane in range(planes):
            out_ref[component, plane] = mixed[:, plane * depth : (plane + 1) * depth]


def cross_parts(left, right):
    return [
        left[1] * right[2] - left[2] * right[1],
        left[2] * right[0] - left[0] * right[2],
        left[0] * right[1] - left[1] * right[0],
    ]


def advance_kernel(table_ref, mask_ref, depth_ref, partial_ref, local_ref, field_ref, *refs):
    in_refs, out_ref, dipole_ref = refs[:-2], refs[-2], refs[-1]
    _, planes, width, depth = out_ref.shape
    for component in range(3):
        mixed = gathered_columns(component, in_refs, mask_ref, table_ref, planes)
        lines = jnp.concatenate(
            [
                mixed[:, plane * depth : (plane + 1) * depth] + partial_ref[component, plane]
                for plane in range(planes)
            ],
            axis=0,
        )
        high, low = split(lines)
        field = product(jnp.concatenate([high, high, low], axis=1), depth_ref[...])
        dipole_ref[component] = field.reshape(planes, width, depth)
    for plane in range(planes):
        moment = [field_ref[component, plane] for component in range(3)]
        effective = [local_ref[c, plane] + dipole_ref[c, plane] for c in range(3)]
        torque = cross_parts(moment, effective)
        twice = cross_parts(moment, torque)
        stepped = [moment[c] - TIME_STEP * (torque[c] + DAMPING * twice[c]) for c in range(3)]
        scale = lax.rsqrt(
            stepped[0] * stepped[0] + stepped[1] * stepped[1] + stepped[2] * stepped[2]
        )
        for component in range(3):
            out_ref[component, plane] = stepped[component] * scale


def local_kernel(scale_ref, field_ref, above_ref, below_ref, bond_ref, noise_ref, out_ref):
    _, planes, width, depth = out_ref.shape
    scale = scale_ref[0]
    for plane in range(planes):
        bonds = [bond_ref[d, plane].astype(jnp.float32) for d in range(3)]
        if plane:
            bond_before = bond_ref[0, plane - 1].astype(jnp.float32)
        for component in range(3):
            value = field_ref[component, plane]
            upper = field_ref[component, plane + 1] if plane + 1 < planes else above_ref[component]
            if plane:
                lower = bond_before * field_ref[component, plane - 1]
            else:
                lower = below_ref[component]
            total = bonds[0] * upper + lower
            total = total + bonds[1] * pltpu.roll(value, width - 1, 0)
            total = total + pltpu.roll(bonds[1] * value, 1, 0)
            total = total + bonds[2] * pltpu.roll(value, depth - 1, 1)
            total = total + pltpu.roll(bonds[2] * value, 1, 1)
            out_ref[component, plane] = total + scale * noise_ref[component, plane].astype(
                jnp.float32
            )


def call(kernel, outs, operands, flops, scratch=(), scalars=0):
    whole = pl.BlockSpec(memory_space=pltpu.VMEM)
    moved = sum(math.prod(a.shape) * a.dtype.itemsize for a in list(operands) + list(outs))
    return pl.pallas_call(
        kernel,
        out_shape=list(outs),
        in_specs=[pl.BlockSpec(memory_space=pltpu.SMEM)] * scalars
        + [whole] * (len(operands) - scalars),
        out_specs=[whole] * len(outs),
        scratch_shapes=list(scratch),
        cost_estimate=pl.CostEstimate(flops=flops, bytes_accessed=moved, transcendentals=0),
        compiler_params=pltpu.CompilerParams(vmem_limit_bytes=VMEM_BYTES),
    )(*operands)


def angles(left, right, length):
    product_of = left[:, None] * right[None, :] % length
    angle = 2.0 * math.pi / length * product_of.astype(jnp.float32)
    return jnp.cos(angle), jnp.sin(angle)


def shape_of(*shape):
    return jax.ShapeDtypeStruct(shape, jnp.float32)


def on_device(moments, couplings, noise, kernel, temps, order, accept):
    planes, width, depth = moments.shape[2:]
    row_block = kernel.shape[2]
    count = lax.axis_size("slab") * lax.axis_size("pen")
    if planes % 8 or row_block % 8 or depth % 128 or count & (count - 1) or moments.shape[0] > 1:
        return plain_on_device(moments, couplings, noise, kernel, temps, order, accept)
    inner = 1 << ((count.bit_length() - 1) // 2)
    outer = count // inner
    half = depth // 2
    rows = row_block // CHUNKS
    me = lax.axis_index(AXES)
    numbers = functools.partial(jnp.arange, dtype=jnp.int32)

    def partner(outer_first):
        near, far = numbers(inner), numbers(outer) * inner
        pair = far[:, None] + near[None, :] if outer_first else far[None, :] + near[:, None]
        return me ^ pair.reshape(-1)

    def spread(block_index, size, start, step):
        return (block_index[:, None] * step + start + numbers(size)[None, :]).reshape(-1)

    lane = numbers(depth)[None, :]
    lower_lane = lane < half
    cosine, sine = angles(numbers(depth), numbers(half), depth)
    middle = (1 - 2 * (numbers(depth) % 2)).astype(jnp.float32)[:, None]
    into_depth = jnp.concatenate([cosine, middle, -sine[:, 1:]], axis=1)
    weight = jnp.where((lane == 0) | (lane == half), 1.0, 2.0) / depth
    out_of_depth = (into_depth * weight).T
    into_depth = table_parts(into_depth.T).T
    out_of_depth = table_parts(out_of_depth.T).T
    into_width, out_of_width, into_masks, out_masks = [], [], [], []
    for chunk in range(CHUNKS):
        wave = spread(partner(True), rows, chunk * rows, row_block)
        cosine, sine = angles(wave, numbers(width), width)
        into_width.append(table_parts(jnp.concatenate([cosine, sine], axis=1)))
        back = jnp.concatenate([cosine, sine], axis=0).T / width
        out_of_width.append(table_parts(back))
        wave = wave[:, None]
        below = (wave > 0) & (wave < width // 2)
        above = wave > width // 2
        ends = (wave == 0) | (wave == width // 2)
        pair = (lane == 0) | (lane == half)
        into_masks.append(
            jnp.stack([below & (lane == half), above & pair]).astype(jnp.float32)
        )
        zero, sign = jnp.zeros((wave.shape[0], depth)), jnp.where(lower_lane, -1.0, 1.0)
        first, last = lane == 0, lane == half
        out_masks.append(
            jnp.stack(
                [
                    jnp.where(pair, jnp.where(ends, 1.0, jnp.where(below & first, 2.0, 0.0)), 1.0)
                    + zero,
                    jnp.where(above & last, 2.0, 0.0) + zero,
                    jnp.where(above & last, -2.0, 0.0) + zero,
                    jnp.where(pair, jnp.where(below & first, -2.0, 0.0), sign) + zero,
                ]
            )
        )
    cell = spread(partner(False), planes, 0, planes)
    cosine, sine = angles(numbers(count * planes), cell, count * planes)
    into_first = table_parts(jnp.concatenate([cosine, sine], axis=1))
    out_of_first = table_parts(
        jnp.concatenate([-cosine.T, sine.T], axis=1) / (count * planes)
    )
    lane = lane[0]
    ends = (me == 0) | (me == count // 2)
    upper = me >= count // 2
    direct = jnp.where(lane == 0, ~upper, jnp.where(lane == half, upper, lane < half))
    direct = direct.astype(jnp.float32)
    pair = ends & ((lane == 0) | (lane == half))
    both = jnp.where(pair, 0.5, 0.0)
    flip = jnp.where(lane == 0, 1.0, -1.0) * both
    kinds = [
        direct,
        1.0 - direct,
        jnp.where(pair, 0.5, direct),
        jnp.where(pair, 0.5, 1.0 - direct),
        flip,
        -flip,
    ]
    weights = jnp.stack(kinds)

    labels = pair_labels(order, accept)
    slot_index = jnp.arange(temps.shape[0], dtype=jnp.int32)
    offset = lax.axis_index("temp")
    own_slots = lax.dynamic_slice_in_dim(slot_index, offset, 1)
    own_labels = lax.dynamic_slice_in_dim(labels, offset, 1)
    scales = (slot_sigma(own_slots, temps), slot_sigma(own_labels, temps))

    kernel_rows = kernel.reshape(6, width * row_block, depth)
    field = moments[0]

    def swap(block, distance):
        if distance == 0:
            return block
        return lax.ppermute(block, AXES, [(i, i ^ distance) for i in range(count)])

    flat = shape_of(3, inner * rows * planes, depth)
    piled = shape_of(outer, 3, rows, planes, depth)
    whole = shape_of(*field.shape)
    far_order = sorted(range(outer), key=lambda i: -(i.bit_length()))
    near_order = range(inner)

    for step_index in range(2):
        above = shifted(field[:, 0], AXES, -1)
        below = shifted(couplings[0, -1].astype(jnp.float32) * field[:, -1], AXES, 1)
        sums = None
        for chunk in range(CHUNKS):
            sent = call(
                forward_kernel,
                [flat] * outer,
                [field, into_depth, into_width[chunk], into_masks[chunk]],
                200_000_000,
            )
            arrived = [None] * outer
            for far in far_order:
                arrived[far] = swap(sent[far], far * inner)
            arrived = [a.reshape(3, inner, rows, planes, depth) for a in arrived]
            spectra = [
                swap(jnp.stack([a[:, near] for a in arrived]), near) for near in near_order
            ]
            spectra = call(
                functools.partial(middle_kernel, chunk * rows, inner),
                [piled] * inner,
                [kernel_rows, weights, into_first, out_of_first]
                + spectra,
                400_000_000,
            )
            spectra = [swap(spectra[near], near) for near in near_order]
            returned = [None] * outer
            for far in far_order:
                block = jnp.stack([s[far] for s in spectra], axis=1).reshape(flat.shape)
                returned[far] = swap(block, far * inner)
            if chunk == 0:
                (sums,) = call(
                    backward_kernel,
                    [whole],
                    [out_of_width[chunk], out_masks[chunk]] + returned,
                    200_000_000,
                )
        (local,) = call(
            local_kernel,
            [whole],
            [scales[step_index], field, above, below, couplings, noise[step_index, 0]],
            20_000_000,
            scalars=1,
        )
        (field,) = call(
            advance_kernel,
            [whole],
            [out_of_width[-1], out_masks[-1], out_of_depth, sums, local, field] + returned,
            300_000_000,
            scratch=[pltpu.VMEM(whole.shape, jnp.float32)],
        )
    return (field[None], labels)


def solution(mesh):
    return jax.shard_map(
        on_device,
        mesh=mesh,
        in_specs=(
            P(("groups", "temp"), None, ("slab", "pen"), None, None),
            P("groups", ("slab", "pen"), None, None),
            P(None, ("groups", "temp"), None, ("slab", "pen"), None, None),
            P(None, None, ("slab", "pen"), None),
            P(),
            P("groups"),
            P("groups"),
        ),
        out_specs=(P(("groups", "temp"), None, ("slab", "pen"), None, None), P("groups")),
        check_vma=False,
    )
```

```python
import functools
import math

import jax
import jax.numpy as jnp
import numpy as np
from jax import lax
from jax.experimental import pallas as pl
from jax.experimental.pallas import tpu as pltpu
from jax.sharding import PartitionSpec as P

TIME_STEP = 0.1
DAMPING = 0.5
AXES = ("slab", "pen")
SCALARS = pl.BlockSpec(memory_space=pltpu.SMEM)


def shifted(block, axis, distance):
    devices = range(lax.axis_size(axis))
    route = [((i - distance) % len(devices), i) for i in devices]
    return lax.ppermute(block, axis, route)


def cross(left, right, axis):
    left_parts = [lax.index_in_dim(left, component, axis, keepdims=False) for component in range(3)]
    right_parts = [
        lax.index_in_dim(right, component, axis, keepdims=False) for component in range(3)
    ]
    result = [
        left_parts[1] * right_parts[2] - left_parts[2] * right_parts[1],
        left_parts[2] * right_parts[0] - left_parts[0] * right_parts[2],
        left_parts[0] * right_parts[1] - left_parts[1] * right_parts[0],
    ]
    return jnp.stack(result, axis=axis)


def pair_labels(order, accept):
    slot_index = jnp.arange(order.shape[0], dtype=jnp.int32)
    position = jnp.sum(
        jnp.where(order[None, :] == slot_index[:, None], slot_index[None, :], 0), axis=1
    )
    mate_position = position + 1 - 2 * (position % 2)
    partner = jnp.sum(
        jnp.where(slot_index[None, :] == mate_position[:, None], order[None, :], 0), axis=1
    )
    partner_flag = jnp.sum(
        jnp.where(slot_index[None, :] == partner[:, None], accept[None, :], 0), axis=1
    )
    accepted = accept * partner_flag
    return jnp.where(accepted == 1, partner, slot_index)


def slot_sigma(labels, temps):
    slot_index = jnp.arange(temps.shape[0], dtype=jnp.int32)
    picked = jnp.sum(
        jnp.where(
            labels[:, None] == slot_index[None, :], temps[None, :], jnp.zeros_like(temps)[None, :]
        ),
        axis=1,
    )
    return jnp.sqrt(2.0 * DAMPING * picked / TIME_STEP)


def angle_tables(length):
    positions = jnp.arange(length, dtype=jnp.int32)
    product = positions[:, None] * positions[None, :] % length
    angles = 2.0 * math.pi / length * product.astype(jnp.float32)
    return (jnp.cos(angles), jnp.sin(angles))


def twist(packed, cosine_table, sine_table, pattern, orientation):
    cosine_part = jnp.einsum(pattern, packed, cosine_table, precision=lax.Precision.HIGHEST)
    sine_part = jnp.einsum(pattern, packed, sine_table, precision=lax.Precision.HIGHEST)
    middle = packed.shape[-1] // 2
    turned = jnp.concatenate([sine_part[..., middle:], -sine_part[..., :middle]], axis=-1)
    return cosine_part + orientation * turned


def pair_twist(stacked, cosine_table, sine_table, pattern, orientation):
    real_part = stacked[:, 0]
    imag_part = stacked[:, 1]
    real_cos = jnp.einsum(pattern, real_part, cosine_table, precision=lax.Precision.HIGHEST)
    real_sin = jnp.einsum(pattern, real_part, sine_table, precision=lax.Precision.HIGHEST)
    imag_cos = jnp.einsum(pattern, imag_part, cosine_table, precision=lax.Precision.HIGHEST)
    imag_sin = jnp.einsum(pattern, imag_part, sine_table, precision=lax.Precision.HIGHEST)
    return jnp.stack([real_cos + orientation * imag_sin, imag_cos - orientation * real_sin], axis=1)


def apply_kernel(spectrum, widened, replicas):
    shaped = spectrum.reshape((replicas, 3) + spectrum.shape[1:])
    comp_one, comp_two, comp_three = (shaped[:, 0], shaped[:, 1], shaped[:, 2])
    result = [
        -(widened[0] * comp_one + widened[3] * comp_two + widened[4] * comp_three),
        -(widened[3] * comp_one + widened[1] * comp_two + widened[5] * comp_three),
        -(widened[4] * comp_one + widened[5] * comp_two + widened[2] * comp_three),
    ]
    return jnp.stack(result, axis=1).reshape(spectrum.shape)


def advance(moment_field, local_field, noise_scale, noise_step):
    effective = local_field + noise_scale[:, None, None, None, None] * noise_step.astype(
        jnp.float32
    )
    torque = cross(moment_field, effective, 1)
    stepped = moment_field - TIME_STEP * (torque + DAMPING * cross(moment_field, torque, 1))
    return stepped * lax.rsqrt(jnp.sum(stepped * stepped, axis=1, keepdims=True))


def neighbor_sum(moment_field, bond_field):
    coupling_first = bond_field[0]
    carried = coupling_first * moment_field
    above = shifted(moment_field[:, :, :1], ("slab", "pen"), -1)
    below = shifted(carried[:, :, -1:], ("slab", "pen"), 1)
    upward = jnp.concatenate([moment_field[:, :, 1:], above], axis=2)
    downward = jnp.concatenate([below, carried[:, :, :-1]], axis=2)
    summed = coupling_first * upward + downward
    for grid_axis in (1, 2):
        coupling = bond_field[grid_axis]
        summed = (
            summed
            + coupling * jnp.roll(moment_field, -1, grid_axis + 2)
            + jnp.roll(coupling * moment_field, 1, grid_axis + 2)
        )
    return summed


def plain_on_device(moments, couplings, noise, kernel, temps, order, accept):
    replicas = moments.shape[0]
    planes = moments.shape[2]
    grid_width = moments.shape[3]
    grid_depth = moments.shape[4]
    slab_count = lax.axis_size("slab")
    pen_count = lax.axis_size("pen")
    slices = slab_count * pen_count
    row_block = grid_width // slices
    channels = 3 * replicas
    low_count = grid_depth // 2
    cosine_depth, sine_depth = angle_tables(grid_depth)
    cosine_width, sine_width = angle_tables(grid_width)
    inverse_cosine = cosine_width / grid_width
    inverse_sine = sine_width / grid_width
    low_weights = jnp.where(jnp.arange(low_count) == 0, 1.0, 2.0).astype(jnp.float32)
    forward_lower = jnp.concatenate(
        [cosine_depth[:, :low_count], -sine_depth[:, :low_count]], axis=1
    )
    backward_lower = (
        jnp.concatenate(
            [
                low_weights[:, None] * cosine_depth[:low_count],
                -low_weights[:, None] * sine_depth[:low_count],
            ],
            axis=0,
        )
        / grid_depth
    )
    kernel_lower = jnp.concatenate([kernel[..., :low_count], kernel[..., :low_count]], axis=-1)
    edge_column = cosine_depth[:, low_count]
    edge_row = cosine_depth[low_count] / grid_depth
    edge_kernel = jnp.swapaxes(kernel[..., low_count], 1, 2)[:, None]
    bond_field = couplings.astype(jnp.float32)
    labels = pair_labels(order, accept)
    slot_index = jnp.arange(temps.shape[0], dtype=jnp.int32)
    offset = lax.axis_index("temp") * replicas
    own_slots = lax.dynamic_slice_in_dim(slot_index, offset, replicas)
    own_labels = lax.dynamic_slice_in_dim(labels, offset, replicas)
    scales = (slot_sigma(own_slots, temps), slot_sigma(own_labels, temps))
    moment_field = moments
    for step_index in range(2):
        flattened = moment_field.reshape(channels, planes, grid_width, grid_depth)
        dipole_lower_part = jnp.dot(flattened, forward_lower, precision=lax.Precision.HIGHEST)
        dipole_lower_part = twist(dipole_lower_part, cosine_width, sine_width, "cxyw,yk->cxkw", 1.0)
        edge = jnp.dot(flattened, edge_column, precision=lax.Precision.HIGHEST)
        edge_real = jnp.einsum("cxy,yk->ckx", edge, cosine_width, precision=lax.Precision.HIGHEST)
        edge_imag = -jnp.einsum("cxy,yk->ckx", edge, sine_width, precision=lax.Precision.HIGHEST)
        edge_edge_in = jnp.stack([edge_real, edge_imag], axis=1).reshape(
            channels, 2, slices, row_block, 1, planes
        )
        edge_edge_moved = lax.all_to_all(
            edge_edge_in, ("slab", "pen"), split_axis=2, concat_axis=4, tiled=True
        )
        dipole_edge_pair = edge_edge_moved.reshape(channels, 2, row_block, grid_width)
        lower_lower_in = dipole_lower_part.reshape(
            channels, 1, planes, slices, row_block, dipole_lower_part.shape[-1]
        )
        lower_lower_out = lax.all_to_all(
            lower_lower_in, ("slab", "pen"), split_axis=3, concat_axis=1, tiled=True
        )
        dipole_lower_part = lower_lower_out.reshape(
            channels, grid_width, row_block, dipole_lower_part.shape[-1]
        )
        dipole_edge_pair = pair_twist(
            dipole_edge_pair, cosine_width, sine_width, "cyx,xk->cyk", 1.0
        )
        dipole_edge_pair = apply_kernel(dipole_edge_pair, edge_kernel, replicas)
        dipole_edge_pair = pair_twist(
            dipole_edge_pair, inverse_cosine, inverse_sine, "cyx,xk->cyk", -1.0
        )
        dipole_lower_part = twist(dipole_lower_part, cosine_width, sine_width, "cxyw,xk->ckyw", 1.0)
        dipole_lower_part = apply_kernel(dipole_lower_part, kernel_lower, replicas)
        dipole_lower_part = twist(
            dipole_lower_part, inverse_cosine, inverse_sine, "cxyw,xk->ckyw", -1.0
        )
        edge_in = dipole_edge_pair.reshape(channels, 2, 1, row_block, slices, planes)
        edge_moved = lax.all_to_all(
            edge_in, ("slab", "pen"), split_axis=4, concat_axis=2, tiled=True
        )
        dipole_edge_pair = edge_moved.reshape(channels, 2, grid_width, planes)
        lower_in = dipole_lower_part.reshape(
            channels, slices, planes, 1, row_block, dipole_lower_part.shape[-1]
        )
        lower_out = lax.all_to_all(
            lower_in, ("slab", "pen"), split_axis=1, concat_axis=3, tiled=True
        )
        dipole_lower_part = lower_out.reshape(
            channels, planes, grid_width, dipole_lower_part.shape[-1]
        )
        dipole_lower_part = twist(
            dipole_lower_part, inverse_cosine, inverse_sine, "cxyw,yk->cxkw", -1.0
        )
        edge_field = jnp.einsum(
            "ckx,ky->cxy", dipole_edge_pair[:, 0], inverse_cosine, precision=lax.Precision.HIGHEST
        ) - jnp.einsum(
            "ckx,ky->cxy", dipole_edge_pair[:, 1], inverse_sine, precision=lax.Precision.HIGHEST
        )
        summed = (
            jnp.dot(dipole_lower_part, backward_lower, precision=lax.Precision.HIGHEST)
            + edge_field[..., None] * edge_row
        )
        local_field = neighbor_sum(moment_field, bond_field) + summed.reshape(moment_field.shape)
        moment_field = advance(moment_field, local_field, scales[step_index], noise[step_index])
    return (moment_field, labels)


def split(value):
    high = value.astype(jnp.bfloat16)
    low = (value - high.astype(jnp.float32)).astype(jnp.bfloat16)
    return high, low


def stacked_parts(value):
    high, low = split(value)
    return jnp.concatenate([high, high, low], axis=0)


def product(left, right):
    return jnp.dot(left, right, preferred_element_type=jnp.float32)


def turn(value):
    return pltpu.roll(value, value.shape[-1] // 2, value.ndim - 1)


def lane_index(shape):
    return lax.broadcasted_iota(jnp.int32, shape, len(shape) - 1)


def forward_kernel(groups, field_ref, depth_ref, *refs):
    table_refs, out_refs = refs[: 2 * len(groups)], refs[2 * len(groups) :]
    _, planes, width, depth = field_ref.shape
    half = depth // 2
    lane = lane_index((width, depth))
    signs = jnp.where(lane == 0, 0.0, jnp.where(lane < half, 1.0, -1.0))
    for component in range(3):
        high, low = split(field_ref[component].reshape(planes * width, depth))
        lines = product(jnp.concatenate([high, high, low], axis=1), depth_ref[...])
        extra = jnp.zeros((width, depth), jnp.float32)
        columns = []
        for plane in range(planes):
            line = lines[plane * width : (plane + 1) * width]
            turned = turn(line)
            moved = pltpu.roll(turned, plane, 1) if plane else turned
            extra = jnp.where(lane == plane, moved, extra)
            columns.append(stacked_parts(jnp.concatenate([line, turned * signs], axis=0)))
        columns.append(stacked_parts(jnp.concatenate([extra, -turn(extra)], axis=0)))
        columns = jnp.concatenate(columns, axis=1)
        outs = list(out_refs)
        for chunk, group in enumerate(groups):
            table_ref, mask_ref = table_refs[2 * chunk : 2 * chunk + 2]
            part = table_ref.shape[0] // group
            mixed = product(table_ref[...], columns)
            extra = mixed[:, planes * depth :]
            for plane in range(planes):
                value = mixed[:, plane * depth : (plane + 1) * depth]
                value = value - mask_ref[0] * pltpu.roll(extra, half - plane, 1)
                back = pltpu.roll(extra, depth - plane, 1) if plane else extra
                value = jnp.where(mask_ref[1] > 0.5, back, value)
                for index, out_ref in enumerate(outs[:group]):
                    out_ref[component, pl.ds(plane, part, stride=planes), :] = value[
                        index * part : (index + 1) * part
                    ]
            outs = outs[group:]


def middle_kernel(start, inner, kernel_ref, weight_ref, table_ref, inverse_ref, *refs):
    in_refs, out_refs = in_order(refs[:inner]), refs[inner:]
    outer, _, rows, planes, depth = in_refs[0].shape
    half = depth // 2
    count = inner * outer * planes
    row_block = kernel_ref.shape[1] // count
    lane = lane_index((count, depth))
    signs = jnp.where(lane < half, 1.0, -1.0)
    order = ((0, 3, 4), (3, 1, 5), (4, 5, 2))
    weights = [weight_ref[i : i + 1, :] for i in range(6)]
    for row in range(rows):
        spectrum, columns = [], []
        edge = start + row == 0
        for component in range(3):
            block = jnp.concatenate(
                [ref[:, component, row].reshape(outer * planes, depth) for ref in in_refs], axis=0
            )
            turned = turn(block)
            columns.append(stacked_parts(jnp.concatenate([block, turned * signs], axis=0)))
            if edge:
                mirror = jnp.concatenate([block * signs, -turned], axis=0)
                spectrum.append(stacked_parts(mirror))
        mixed = product(table_ref[...], jnp.concatenate(columns + spectrum, axis=1))
        spectrum = [mixed[:, i * depth : (i + 1) * depth] for i in range(mixed.shape[1] // depth)]
        totals = [None] * 3
        for entry in range(6):
            raw = kernel_ref[entry, pl.ds(start + row, count, stride=row_block), :]
            raw_turned = turn(raw)
            pick = 2 if edge else 0
            value = raw * weights[pick] + raw_turned * weights[pick + 1]
            for i in range(3):
                for j in range(3):
                    if order[i][j] == entry:
                        term = value * spectrum[j]
                        totals[i] = term if totals[i] is None else totals[i] + term
            if edge:
                value = raw * weights[4] + raw_turned * weights[5]
                for i in range(3):
                    for j in range(3):
                        if order[i][j] == entry:
                            totals[i] = totals[i] + value * spectrum[3 + j]
        columns = [
            stacked_parts(jnp.concatenate([total, turn(total) * signs], axis=0)) for total in totals
        ]
        mixed = product(inverse_ref[...], jnp.concatenate(columns, axis=1))
        for component in range(3):
            value = mixed[:, component * depth : (component + 1) * depth]
            for index, out_ref in enumerate(out_refs):
                size = outer * planes
                out_ref[:, component, row] = value[index * size : (index + 1) * size].reshape(
                    outer, planes, depth
                )


def gathered_columns(component, in_refs, mask_ref, table_ref, planes):
    part = in_refs[0].shape[1] // planes
    columns = []
    for plane in range(planes):
        value = jnp.concatenate(
            [ref[component, pl.ds(plane, part, stride=planes), :] for ref in in_refs], axis=0
        )
        turned = turn(value)
        top = value * mask_ref[0] + turned * mask_ref[1]
        bottom = value * mask_ref[2] + turned * mask_ref[3]
        columns.append(stacked_parts(jnp.concatenate([top, bottom], axis=0)))
    return product(table_ref[...], jnp.concatenate(columns, axis=1))


def backward_kernel(table_ref, mask_ref, *refs):
    in_refs, out_ref = in_order(refs[:-1]), refs[-1]
    _, planes, _, depth = out_ref.shape
    for component in range(3):
        mixed = gathered_columns(component, in_refs, mask_ref, table_ref, planes)
        for plane in range(planes):
            out_ref[component, plane] = mixed[:, plane * depth : (plane + 1) * depth]


def cross_parts(left, right):
    return [
        left[1] * right[2] - left[2] * right[1],
        left[2] * right[0] - left[0] * right[2],
        left[0] * right[1] - left[1] * right[0],
    ]


def edge_planes(field_ref, bond_ref, first_ref, carried_ref):
    bond = bond_ref[0, 0].astype(jnp.float32)
    for component in range(3):
        first_ref[component] = field_ref[component, 0]
        carried_ref[component] = bond * field_ref[component, field_ref.shape[1] - 1]


def advance_kernel(edges, *refs):
    refs, (out_ref, *edge_refs, dipole_ref) = refs[: -2 - 2 * edges], refs[-2 - 2 * edges :]
    in_refs, refs = in_order(refs[:-7]), refs[-7:]
    table_ref, mask_ref, depth_ref, partial_ref, local_ref, field_ref, bond_ref = refs
    _, planes, width, depth = out_ref.shape
    for component in range(3):
        mixed = gathered_columns(component, in_refs, mask_ref, table_ref, planes)
        lines = jnp.concatenate(
            [
                mixed[:, plane * depth : (plane + 1) * depth] + partial_ref[component, plane]
                for plane in range(planes)
            ],
            axis=0,
        )
        high, low = split(lines)
        field = product(jnp.concatenate([high, high, low], axis=1), depth_ref[...])
        dipole_ref[component] = field.reshape(planes, width, depth)
    for plane in range(planes):
        moment = [field_ref[component, plane] for component in range(3)]
        effective = [local_ref[c, plane] + dipole_ref[c, plane] for c in range(3)]
        torque = cross_parts(moment, effective)
        twice = cross_parts(moment, torque)
        stepped = [moment[c] - TIME_STEP * (torque[c] + DAMPING * twice[c]) for c in range(3)]
        scale = lax.rsqrt(
            stepped[0] * stepped[0] + stepped[1] * stepped[1] + stepped[2] * stepped[2]
        )
        for component in range(3):
            out_ref[component, plane] = stepped[component] * scale
    if edges:
        edge_planes(out_ref, bond_ref, *edge_refs)


def local_kernel(
    step, scale_ref, field_ref, above_ref, below_ref, bond_ref, noise_ref, out_ref, held_ref, sem
):
    _, planes, width, depth = out_ref.shape
    copy = pltpu.make_async_copy(noise_ref.at[step], held_ref, sem)
    copy.start()
    copy.wait()
    scale = scale_ref[step : step + 1, :]
    for plane in range(planes):
        bonds = [bond_ref[d, plane].astype(jnp.float32) for d in range(3)]
        if plane:
            bond_before = bond_ref[0, plane - 1].astype(jnp.float32)
        for component in range(3):
            value = field_ref[component, plane]
            upper = field_ref[component, plane + 1] if plane + 1 < planes else above_ref[component]
            if plane:
                lower = bond_before * field_ref[component, plane - 1]
            else:
                lower = below_ref[component]
            total = bonds[0] * upper + lower
            total = total + bonds[1] * pltpu.roll(value, width - 1, 0)
            total = total + pltpu.roll(bonds[1] * value, 1, 0)
            total = total + bonds[2] * pltpu.roll(value, depth - 1, 1)
            total = total + pltpu.roll(bonds[2] * value, 1, 1)
            out_ref[component, plane] = total + scale * held_ref[component, plane].astype(
                jnp.float32
            )


def call(kernel, outs, operands, scratch=(), specs=None, out_specs=None, before=(), after=(), mib=16):
    specs = {} if specs is None else specs
    out_specs = {} if out_specs is None else out_specs
    whole = pl.BlockSpec(memory_space=pltpu.VMEM)
    unread = pl.BlockSpec(memory_space=pl.ANY)

    def body(*refs):
        refs = refs[len(before) :]
        kernel(*refs[: len(operands)], *refs[len(operands) + len(after) :])

    return pl.pallas_call(
        body,
        out_shape=list(outs),
        in_specs=[unread] * len(before)
        + [specs.get(i, whole) for i in range(len(operands))]
        + [unread] * len(after),
        out_specs=[out_specs.get(i, whole) for i in range(len(outs))],
        scratch_shapes=list(scratch),
        cost_estimate=pl.CostEstimate(flops=1, bytes_accessed=1, transcendentals=0),
        compiler_params=pltpu.CompilerParams(vmem_limit_bytes=mib * 1024 * 1024),
    )(*before, *operands, *after)


def shape_of(*shape, dtype=jnp.float32):
    return jax.ShapeDtypeStruct(shape, dtype)


def log2(size):
    return size.bit_length() - 1


class Route:
    def __init__(self, start, rows, first, second):
        self.start, self.rows, self.first, self.second = start, rows, first, second

    def distance(self, index, second_leads):
        lead, last = (self.second, self.first) if second_leads else (self.first, self.second)
        return (index >> log2(last[0])) * lead[1] + (index & (last[0] - 1)) * last[1]

    def waves(self, me, index, row_block):
        block = me ^ self.distance(index >> log2(self.rows), False)
        return block * row_block + self.start + (index & (self.rows - 1))

    def cells(self, me, index, planes):
        block = me ^ self.distance(index >> log2(planes), True)
        return block * planes + (index & (planes - 1))


def angles(left, right, length):
    angle = (2.0 * math.pi / length) * ((left * right) & (length - 1)).astype(jnp.float32)
    return jnp.cos(angle), jnp.sin(angle)


def table_parts(table):
    high, low = split(table)
    return jnp.concatenate([high, low, high], axis=1)


def iota(shape, axis):
    return lax.broadcasted_iota(jnp.int32, shape, axis)


def forward_tables(routes, row_block, me_ref, *out_refs):
    me = me_ref[0]
    for route, table_ref, mask_ref in zip(routes, out_refs[0::2], out_refs[1::2]):
        _, count, depth = mask_ref.shape
        width = table_ref.shape[1] // 6
        wave = route.waves(me, iota((count, width), 0), row_block)
        cosine, sine = angles(wave, iota((count, width), 1), width)
        table_ref[...] = table_parts(jnp.concatenate([cosine, sine], axis=1))
        wave = route.waves(me, iota((count, depth), 0), row_block)
        lane = iota((count, depth), 1)
        below = (wave > 0) & (wave < width // 2) & (lane == depth // 2)
        above = (wave > width // 2) & ((lane == 0) | (lane == depth // 2))
        mask_ref[0] = jnp.where(below, 1.0, 0.0)
        mask_ref[1] = jnp.where(above, 1.0, 0.0)


def other_tables(routes, row_block, planes, me_ref, temps_ref, order_ref, accept_ref, *out_refs):
    labels_ref, scale_ref, weight_ref, *out_refs = out_refs
    me = me_ref[0]
    for pair in range(order_ref.shape[0] // 2):
        left, right = order_ref[2 * pair], order_ref[2 * pair + 1]
        swapped = (accept_ref[left] == 1) & (accept_ref[right] == 1)
        labels_ref[left] = jnp.where(swapped, right, left)
        labels_ref[right] = jnp.where(swapped, left, right)
    for step, slot in enumerate((me_ref[1], labels_ref[me_ref[1]])):
        picked = jnp.full((1, scale_ref.shape[1]), temps_ref[slot], jnp.float32)
        scale_ref[step : step + 1, :] = jnp.sqrt(2.0 * DAMPING * picked / TIME_STEP)
    depth = weight_ref.shape[1]
    half = depth // 2
    for index, route in enumerate(routes):
        into_ref, out_ref, table_ref, mask_ref = out_refs[4 * index : 4 * index + 4]
        cells = into_ref.shape[0]
        shape = (cells, cells)
        cosine, sine = angles(route.cells(me, iota(shape, 1), planes), iota(shape, 0), cells)
        into_ref[...] = table_parts(jnp.concatenate([cosine, sine], axis=1))
        cosine, sine = angles(route.cells(me, iota(shape, 0), planes), iota(shape, 1), cells)
        out_ref[...] = table_parts(jnp.concatenate([-cosine, sine], axis=1) / cells)
        count = mask_ref.shape[1]
        width = table_ref.shape[0]
        shape = (width, count)
        wave = route.waves(me, iota(shape, 1), row_block)
        cosine, sine = angles(wave, iota(shape, 0), width)
        table_ref[...] = table_parts(jnp.concatenate([cosine, sine], axis=1) / width)
        shape = (count, depth)
        wave = route.waves(me, iota(shape, 0), row_block)
        lane = iota(shape, 1)
        first, last = lane == 0, lane == half
        pair = first | last
        below = (wave > 0) & (wave < width // 2) & first
        above = (wave > width // 2) & last
        ends = (wave == 0) | (wave == width // 2)
        sign = jnp.where(lane < half, -1.0, 1.0)
        mask_ref[0] = jnp.where(pair, jnp.where(ends, 1.0, jnp.where(below, 2.0, 0.0)), 1.0)
        mask_ref[1] = jnp.where(above, 2.0, 0.0)
        mask_ref[2] = jnp.where(above, -2.0, 0.0)
        mask_ref[3] = jnp.where(pair, jnp.where(below, -2.0, 0.0), sign)
    blocks = width // row_block
    ends = jnp.where((me & (blocks // 2 - 1)) == 0, 1.0, 0.0)
    upper = jnp.where(me >= blocks // 2, 1.0, 0.0)
    lane = iota((1, depth), 1)
    first, last = lane == 0, lane == half
    direct = jnp.where(first, 1.0 - upper, jnp.where(last, upper, jnp.where(lane < half, 1.0, 0.0)))
    both = jnp.where(first | last, 0.5 * ends, 0.0)
    keep = jnp.where(first | last, 1.0 - ends, 1.0)
    flip = jnp.where(first, both, -both)
    kinds = [
        direct,
        1.0 - direct,
        direct * keep + both,
        (1.0 - direct) * keep + both,
        flip,
        -flip,
    ]
    for index, kind in enumerate(kinds):
        weight_ref[index : index + 1, :] = kind


def visiting(count):
    return sorted(range(count), key=lambda i: (i < count // 2, i))


def in_order(refs):
    ordered = [None] * len(refs)
    for place, ref in zip(visiting(len(refs)), refs):
        ordered[place] = ref
    return ordered


def leaving(blocks):
    return [blocks[i] for i in visiting(len(blocks))]


def repack_forward(count, *refs):
    in_refs, out_refs = in_order(refs[:count]), refs[count:]
    for out_index, out_ref in enumerate(out_refs):
        for in_index, in_ref in enumerate(in_refs):
            out_ref[in_index] = in_ref[:, out_index]


def repack_backward(count, *refs):
    in_refs, out_refs = in_order(refs[:count]), refs[count:]
    for out_index, out_ref in enumerate(out_refs):
        for in_index, in_ref in enumerate(in_refs):
            out_ref[:, in_index] = in_ref[out_index]


def depth_tables(depth):
    half = depth // 2
    angle = 2.0 * np.pi / depth * np.outer(np.arange(depth), np.arange(half)) % (2.0 * np.pi)
    middle = np.where(np.arange(depth) % 2 == 0, 1.0, -1.0)[:, None]
    into = np.concatenate([np.cos(angle), middle, -np.sin(angle[:, 1:])], axis=1)
    lane = np.arange(depth)
    out_of = (into * np.where(lane % half == 0, 1.0, 2.0) / depth).T
    tables = []
    for table in (into, out_of):
        high = table.astype(jnp.bfloat16)
        low = (table - high.astype(np.float64)).astype(jnp.bfloat16)
        tables.append(jnp.asarray(np.concatenate([high, low, high], axis=0)))
    return tables


def on_device(moments, couplings, noise, kernel, temps, order, accept):
    planes, width, depth = moments.shape[2:]
    row_block = kernel.shape[2]
    count = lax.axis_size("slab") * lax.axis_size("pen")
    if planes % 8 or row_block % 8 or depth % 128 or count & (count - 1) or moments.shape[0] > 1:
        return plain_on_device(moments, couplings, noise, kernel, temps, order, accept)
    near = (1 << (log2(count) // 2), 1)
    far = (count // near[0], near[0])
    rows = row_block // 2
    routes = [Route(0, rows, far, near), Route(rows, rows, near, far)]
    me = jnp.stack([lax.axis_index(AXES), lax.axis_index("temp")]).astype(jnp.int32)
    into_depth, out_of_depth = depth_tables(depth)
    lines = count * rows
    field = moments[0]
    whole = shape_of(*field.shape)
    plane_shape = shape_of(3, width, depth)
    forward = call(
        functools.partial(forward_tables, routes, row_block),
        [shape_of(lines, 6 * width, dtype=jnp.bfloat16), shape_of(2, lines, depth)] * 2,
        [me],
        specs={0: SCALARS},
    )
    square = shape_of(width, 6 * width, dtype=jnp.bfloat16)
    labels, scales, weights, *others = call(
        functools.partial(other_tables, routes, row_block, planes),
        [shape_of(*order.shape, dtype=jnp.int32), shape_of(2, depth), shape_of(6, depth)]
        + [square, square, shape_of(width, 6 * lines, dtype=jnp.bfloat16), shape_of(4, lines, depth)]
        * 2,
        [me, temps, order, accept],
        specs={i: SCALARS for i in range(4)},
        out_specs={0: SCALARS},
    )
    others = [others[:4], others[4:]]
    kernel_rows = kernel.reshape(6, width * row_block, depth)
    noise = noise[:, 0]
    unread = pl.BlockSpec(memory_space=pl.ANY)

    def exchange(blocks, stage):
        size, stride = stage
        moved = list(blocks)
        for index in leaving(range(size)):
            if not index:
                continue
            distance = index * stride
            moved[index] = lax.ppermute(
                blocks[index], AXES, [(i, i ^ distance) for i in range(count)]
            )
        return moved

    def forward_part(field):
        groups = [route.first[0] for route in routes]
        outs = []
        for route in routes:
            shape = shape_of(3, route.second[0] * rows * planes, depth)
            outs += [shape] * route.first[0]
        blocks = call(
            functools.partial(forward_kernel, groups),
            outs,
            [field, into_depth, *forward],
        )
        return blocks[: groups[0]], blocks[groups[0] :]

    def forward_repack(chunk, blocks, **order):
        first, second = routes[chunk].first[0], routes[chunk].second[0]
        return call(
            functools.partial(repack_forward, first),
            [shape_of(first, 3, rows * planes, depth)] * second,
            [block.reshape(3, second, rows * planes, depth) for block in leaving(blocks)],
            **order,
        )

    def middle_part(chunk, blocks, **order):
        first, second = routes[chunk].first[0], routes[chunk].second[0]
        into_first, out_of_first = others[chunk][:2]
        shape = shape_of(first, 3, rows, planes, depth)
        return call(
            functools.partial(middle_kernel, routes[chunk].start, second),
            [shape] * second,
            [kernel_rows, weights, into_first, out_of_first]
            + [block.reshape(shape.shape) for block in leaving(blocks)],
            **order,
        )

    def backward_repack(chunk, blocks, **order):
        first, second = routes[chunk].first[0], routes[chunk].second[0]
        blocks = call(
            functools.partial(repack_backward, second),
            [shape_of(3, second, rows * planes, depth)] * first,
            [block.reshape(first, 3, rows * planes, depth) for block in leaving(blocks)],
            **order,
        )
        return [block.reshape(3, -1, depth) for block in blocks]

    first_plane = field[:, 0]
    carried = couplings[0, -1].astype(jnp.float32) * field[:, -1]
    for step in range(2):
        a_out, b_out = forward_part(field)
        a_far = exchange(a_out, far)
        b_near = exchange(b_out, near)
        b_packed = forward_repack(1, b_near)
        a_packed = forward_repack(0, a_far, after=b_packed[:1])
        b_far = exchange(b_packed, far)
        a_near = exchange(a_packed, near)
        a_mid = middle_part(0, a_near)
        b_mid = middle_part(1, b_far, before=a_mid[:1])
        above = shifted(first_plane, AXES, -1)
        below = shifted(carried, AXES, 1)
        b_back = exchange(b_mid, far)
        a_back = exchange(a_mid, near)
        a_home = backward_repack(0, a_back, before=b_mid[:1], after=[above, below])
        b_home = backward_repack(1, b_back, before=a_home[:1])
        a_done = exchange(a_home, far)
        b_done = exchange(b_home, near)
        (local,) = call(
            functools.partial(local_kernel, step),
            [whole],
            [scales, field, above, below, couplings, noise],
            scratch=[pltpu.VMEM(field.shape, noise.dtype), pltpu.SemaphoreType.DMA(())],
            specs={5: unread},
            before=a_home[:1],
        )
        (sums,) = call(
            backward_kernel,
            [whole],
            [others[1][2], others[1][3]] + leaving(b_done),
            after=[local],
        )
        edges = step == 0
        field, *planes_out = call(
            functools.partial(advance_kernel, edges),
            [whole] + [plane_shape] * 2 * edges,
            leaving(a_done)
            + [others[0][2], others[0][3], out_of_depth, sums, local, field, couplings[:1, -1:]],
            scratch=[pltpu.VMEM(whole.shape, jnp.float32)],
        )
        if edges:
            first_plane, carried = planes_out
    return (field[None], labels)


def solution(mesh):
    return jax.shard_map(
        on_device,
        mesh=mesh,
        in_specs=(
            P(("groups", "temp"), None, ("slab", "pen"), None, None),
            P("groups", ("slab", "pen"), None, None),
            P(None, ("groups", "temp"), None, ("slab", "pen"), None, None),
            P(None, None, ("slab", "pen"), None),
            P(),
            P("groups"),
            P("groups"),
        ),
        out_specs=(P(("groups", "temp"), None, ("slab", "pen"), None, None), P("groups")),
        check_vma=False,
    )
```

```python
import functools
import math

import jax
import jax.numpy as jnp
import numpy as np
from jax import lax
from jax.experimental import pallas as pl
from jax.experimental.pallas import tpu as pltpu
from jax.sharding import PartitionSpec as P

TIME_STEP = 0.1
DAMPING = 0.5
AXES = ("slab", "pen")
FAR_ORDER = (3, 1, 2, 0)
NEAR_ORDER = (2, 3, 1, 0)
FAR_EXTRA = (0, 1, 1, 1)
NEAR_EXTRA = (0, 0, 0, 0)
SCALARS = pl.BlockSpec(memory_space=pltpu.SMEM)


def shifted(block, axis, distance):
    devices = range(lax.axis_size(axis))
    route = [((i - distance) % len(devices), i) for i in devices]
    return lax.ppermute(block, axis, route)


def cross(left, right, axis):
    left_parts = [lax.index_in_dim(left, component, axis, keepdims=False) for component in range(3)]
    right_parts = [
        lax.index_in_dim(right, component, axis, keepdims=False) for component in range(3)
    ]
    result = [
        left_parts[1] * right_parts[2] - left_parts[2] * right_parts[1],
        left_parts[2] * right_parts[0] - left_parts[0] * right_parts[2],
        left_parts[0] * right_parts[1] - left_parts[1] * right_parts[0],
    ]
    return jnp.stack(result, axis=axis)


def pair_labels(order, accept):
    slot_index = jnp.arange(order.shape[0], dtype=jnp.int32)
    position = jnp.sum(
        jnp.where(order[None, :] == slot_index[:, None], slot_index[None, :], 0), axis=1
    )
    mate_position = position + 1 - 2 * (position % 2)
    partner = jnp.sum(
        jnp.where(slot_index[None, :] == mate_position[:, None], order[None, :], 0), axis=1
    )
    partner_flag = jnp.sum(
        jnp.where(slot_index[None, :] == partner[:, None], accept[None, :], 0), axis=1
    )
    accepted = accept * partner_flag
    return jnp.where(accepted == 1, partner, slot_index)


def slot_sigma(labels, temps):
    slot_index = jnp.arange(temps.shape[0], dtype=jnp.int32)
    picked = jnp.sum(
        jnp.where(
            labels[:, None] == slot_index[None, :], temps[None, :], jnp.zeros_like(temps)[None, :]
        ),
        axis=1,
    )
    return jnp.sqrt(2.0 * DAMPING * picked / TIME_STEP)


def angle_tables(length):
    positions = jnp.arange(length, dtype=jnp.int32)
    product = positions[:, None] * positions[None, :] % length
    angles = 2.0 * math.pi / length * product.astype(jnp.float32)
    return (jnp.cos(angles), jnp.sin(angles))


def twist(packed, cosine_table, sine_table, pattern, orientation):
    cosine_part = jnp.einsum(pattern, packed, cosine_table, precision=lax.Precision.HIGHEST)
    sine_part = jnp.einsum(pattern, packed, sine_table, precision=lax.Precision.HIGHEST)
    middle = packed.shape[-1] // 2
    turned = jnp.concatenate([sine_part[..., middle:], -sine_part[..., :middle]], axis=-1)
    return cosine_part + orientation * turned


def pair_twist(stacked, cosine_table, sine_table, pattern, orientation):
    real_part = stacked[:, 0]
    imag_part = stacked[:, 1]
    real_cos = jnp.einsum(pattern, real_part, cosine_table, precision=lax.Precision.HIGHEST)
    real_sin = jnp.einsum(pattern, real_part, sine_table, precision=lax.Precision.HIGHEST)
    imag_cos = jnp.einsum(pattern, imag_part, cosine_table, precision=lax.Precision.HIGHEST)
    imag_sin = jnp.einsum(pattern, imag_part, sine_table, precision=lax.Precision.HIGHEST)
    return jnp.stack([real_cos + orientation * imag_sin, imag_cos - orientation * real_sin], axis=1)


def apply_kernel(spectrum, widened, replicas):
    shaped = spectrum.reshape((replicas, 3) + spectrum.shape[1:])
    comp_one, comp_two, comp_three = (shaped[:, 0], shaped[:, 1], shaped[:, 2])
    result = [
        -(widened[0] * comp_one + widened[3] * comp_two + widened[4] * comp_three),
        -(widened[3] * comp_one + widened[1] * comp_two + widened[5] * comp_three),
        -(widened[4] * comp_one + widened[5] * comp_two + widened[2] * comp_three),
    ]
    return jnp.stack(result, axis=1).reshape(spectrum.shape)


def advance(moment_field, local_field, noise_scale, noise_step):
    effective = local_field + noise_scale[:, None, None, None, None] * noise_step.astype(
        jnp.float32
    )
    torque = cross(moment_field, effective, 1)
    stepped = moment_field - TIME_STEP * (torque + DAMPING * cross(moment_field, torque, 1))
    return stepped * lax.rsqrt(jnp.sum(stepped * stepped, axis=1, keepdims=True))


def neighbor_sum(moment_field, bond_field):
    coupling_first = bond_field[0]
    carried = coupling_first * moment_field
    above = shifted(moment_field[:, :, :1], ("slab", "pen"), -1)
    below = shifted(carried[:, :, -1:], ("slab", "pen"), 1)
    upward = jnp.concatenate([moment_field[:, :, 1:], above], axis=2)
    downward = jnp.concatenate([below, carried[:, :, :-1]], axis=2)
    summed = coupling_first * upward + downward
    for grid_axis in (1, 2):
        coupling = bond_field[grid_axis]
        summed = (
            summed
            + coupling * jnp.roll(moment_field, -1, grid_axis + 2)
            + jnp.roll(coupling * moment_field, 1, grid_axis + 2)
        )
    return summed


def plain_on_device(moments, couplings, noise, kernel, temps, order, accept):
    replicas = moments.shape[0]
    planes = moments.shape[2]
    grid_width = moments.shape[3]
    grid_depth = moments.shape[4]
    slab_count = lax.axis_size("slab")
    pen_count = lax.axis_size("pen")
    slices = slab_count * pen_count
    row_block = grid_width // slices
    channels = 3 * replicas
    low_count = grid_depth // 2
    cosine_depth, sine_depth = angle_tables(grid_depth)
    cosine_width, sine_width = angle_tables(grid_width)
    inverse_cosine = cosine_width / grid_width
    inverse_sine = sine_width / grid_width
    low_weights = jnp.where(jnp.arange(low_count) == 0, 1.0, 2.0).astype(jnp.float32)
    forward_lower = jnp.concatenate(
        [cosine_depth[:, :low_count], -sine_depth[:, :low_count]], axis=1
    )
    backward_lower = (
        jnp.concatenate(
            [
                low_weights[:, None] * cosine_depth[:low_count],
                -low_weights[:, None] * sine_depth[:low_count],
            ],
            axis=0,
        )
        / grid_depth
    )
    kernel_lower = jnp.concatenate([kernel[..., :low_count], kernel[..., :low_count]], axis=-1)
    edge_column = cosine_depth[:, low_count]
    edge_row = cosine_depth[low_count] / grid_depth
    edge_kernel = jnp.swapaxes(kernel[..., low_count], 1, 2)[:, None]
    bond_field = couplings.astype(jnp.float32)
    labels = pair_labels(order, accept)
    slot_index = jnp.arange(temps.shape[0], dtype=jnp.int32)
    offset = lax.axis_index("temp") * replicas
    own_slots = lax.dynamic_slice_in_dim(slot_index, offset, replicas)
    own_labels = lax.dynamic_slice_in_dim(labels, offset, replicas)
    scales = (slot_sigma(own_slots, temps), slot_sigma(own_labels, temps))
    moment_field = moments
    for step_index in range(2):
        flattened = moment_field.reshape(channels, planes, grid_width, grid_depth)
        dipole_lower_part = jnp.dot(flattened, forward_lower, precision=lax.Precision.HIGHEST)
        dipole_lower_part = twist(dipole_lower_part, cosine_width, sine_width, "cxyw,yk->cxkw", 1.0)
        edge = jnp.dot(flattened, edge_column, precision=lax.Precision.HIGHEST)
        edge_real = jnp.einsum("cxy,yk->ckx", edge, cosine_width, precision=lax.Precision.HIGHEST)
        edge_imag = -jnp.einsum("cxy,yk->ckx", edge, sine_width, precision=lax.Precision.HIGHEST)
        edge_edge_in = jnp.stack([edge_real, edge_imag], axis=1).reshape(
            channels, 2, slices, row_block, 1, planes
        )
        edge_edge_moved = lax.all_to_all(
            edge_edge_in, ("slab", "pen"), split_axis=2, concat_axis=4, tiled=True
        )
        dipole_edge_pair = edge_edge_moved.reshape(channels, 2, row_block, grid_width)
        lower_lower_in = dipole_lower_part.reshape(
            channels, 1, planes, slices, row_block, dipole_lower_part.shape[-1]
        )
        lower_lower_out = lax.all_to_all(
            lower_lower_in, ("slab", "pen"), split_axis=3, concat_axis=1, tiled=True
        )
        dipole_lower_part = lower_lower_out.reshape(
            channels, grid_width, row_block, dipole_lower_part.shape[-1]
        )
        dipole_edge_pair = pair_twist(
            dipole_edge_pair, cosine_width, sine_width, "cyx,xk->cyk", 1.0
        )
        dipole_edge_pair = apply_kernel(dipole_edge_pair, edge_kernel, replicas)
        dipole_edge_pair = pair_twist(
            dipole_edge_pair, inverse_cosine, inverse_sine, "cyx,xk->cyk", -1.0
        )
        dipole_lower_part = twist(dipole_lower_part, cosine_width, sine_width, "cxyw,xk->ckyw", 1.0)
        dipole_lower_part = apply_kernel(dipole_lower_part, kernel_lower, replicas)
        dipole_lower_part = twist(
            dipole_lower_part, inverse_cosine, inverse_sine, "cxyw,xk->ckyw", -1.0
        )
        edge_in = dipole_edge_pair.reshape(channels, 2, 1, row_block, slices, planes)
        edge_moved = lax.all_to_all(
            edge_in, ("slab", "pen"), split_axis=4, concat_axis=2, tiled=True
        )
        dipole_edge_pair = edge_moved.reshape(channels, 2, grid_width, planes)
        lower_in = dipole_lower_part.reshape(
            channels, slices, planes, 1, row_block, dipole_lower_part.shape[-1]
        )
        lower_out = lax.all_to_all(
            lower_in, ("slab", "pen"), split_axis=1, concat_axis=3, tiled=True
        )
        dipole_lower_part = lower_out.reshape(
            channels, planes, grid_width, dipole_lower_part.shape[-1]
        )
        dipole_lower_part = twist(
            dipole_lower_part, inverse_cosine, inverse_sine, "cxyw,yk->cxkw", -1.0
        )
        edge_field = jnp.einsum(
            "ckx,ky->cxy", dipole_edge_pair[:, 0], inverse_cosine, precision=lax.Precision.HIGHEST
        ) - jnp.einsum(
            "ckx,ky->cxy", dipole_edge_pair[:, 1], inverse_sine, precision=lax.Precision.HIGHEST
        )
        summed = (
            jnp.dot(dipole_lower_part, backward_lower, precision=lax.Precision.HIGHEST)
            + edge_field[..., None] * edge_row
        )
        local_field = neighbor_sum(moment_field, bond_field) + summed.reshape(moment_field.shape)
        moment_field = advance(moment_field, local_field, scales[step_index], noise[step_index])
    return (moment_field, labels)


def split(value):
    high = value.astype(jnp.bfloat16)
    low = (value - high.astype(jnp.float32)).astype(jnp.bfloat16)
    return high, low


def stacked_parts(value):
    high, low = split(value)
    return jnp.concatenate([high, high, low], axis=0)


def product(left, right):
    return jnp.dot(left, right, preferred_element_type=jnp.float32)


def turn(value):
    return pltpu.roll(value, value.shape[-1] // 2, value.ndim - 1)


def lane_index(shape):
    return lax.broadcasted_iota(jnp.int32, shape, len(shape) - 1)


def forward_kernel(groups, field_ref, depth_ref, *refs):
    table_refs, out_refs = refs[: 2 * len(groups)], refs[2 * len(groups) :]
    _, planes, width, depth = field_ref.shape
    half = depth // 2
    lane = lane_index((width, depth))
    signs = jnp.where(lane == 0, 0.0, jnp.where(lane < half, 1.0, -1.0))
    for component in range(3):
        high, low = split(field_ref[component].reshape(planes * width, depth))
        lines = product(jnp.concatenate([high, high, low], axis=1), depth_ref[...])
        extra = jnp.zeros((width, depth), jnp.float32)
        columns = []
        for plane in range(planes):
            line = lines[plane * width : (plane + 1) * width]
            turned = turn(line)
            moved = pltpu.roll(turned, plane, 1) if plane else turned
            extra = jnp.where(lane == plane, moved, extra)
            columns.append(stacked_parts(jnp.concatenate([line, turned * signs], axis=0)))
        columns.append(stacked_parts(jnp.concatenate([extra, -turn(extra)], axis=0)))
        columns = jnp.concatenate(columns, axis=1)
        outs = list(out_refs)
        for chunk, group in enumerate(groups):
            table_ref, mask_ref = table_refs[2 * chunk : 2 * chunk + 2]
            part = table_ref.shape[0] // group
            mixed = product(table_ref[...], columns)
            extra = mixed[:, planes * depth :]
            for plane in range(planes):
                value = mixed[:, plane * depth : (plane + 1) * depth]
                value = value - mask_ref[0] * pltpu.roll(extra, half - plane, 1)
                back = pltpu.roll(extra, depth - plane, 1) if plane else extra
                value = jnp.where(mask_ref[1] > 0.5, back, value)
                start = component * part * planes + plane
                for index, out_ref in enumerate(outs[:group]):
                    out_ref[pl.ds(start, part, stride=planes), :] = value[
                        index * part : (index + 1) * part
                    ]
            outs = outs[group:]


def middle_kernel(start, rows, inner, planes, kernel_ref, weight_ref, table_ref, inverse_ref, *refs):
    in_refs, out_refs = refs[:inner], refs[inner:]
    count, depth = table_ref.shape[0], weight_ref.shape[1]
    half = depth // 2
    outer = count // (inner * planes)
    row_block = kernel_ref.shape[1] // count

    def places(component, row):
        return [((far * 3 + component) * rows + row) * planes for far in range(outer)]

    lane = lane_index((count, depth))
    signs = jnp.where(lane < half, 1.0, -1.0)
    order = ((0, 3, 4), (3, 1, 5), (4, 5, 2))
    weights = [weight_ref[i : i + 1, :] for i in range(6)]
    for row in range(rows):
        spectrum, columns = [], []
        edge = start + row == 0
        for component in range(3):
            block = jnp.concatenate(
                [
                    ref[place : place + planes, :]
                    for ref in in_refs
                    for place in places(component, row)
                ],
                axis=0,
            )
            turned = turn(block)
            columns.append(stacked_parts(jnp.concatenate([block, turned * signs], axis=0)))
            if edge:
                mirror = jnp.concatenate([block * signs, -turned], axis=0)
                spectrum.append(stacked_parts(mirror))
        mixed = product(table_ref[...], jnp.concatenate(columns + spectrum, axis=1))
        spectrum = [mixed[:, i * depth : (i + 1) * depth] for i in range(mixed.shape[1] // depth)]
        totals = [None] * 3
        for entry in range(6):
            raw = kernel_ref[entry, pl.ds(start + row, count, stride=row_block), :]
            raw_turned = turn(raw)
            pick = 2 if edge else 0
            value = raw * weights[pick] + raw_turned * weights[pick + 1]
            for i in range(3):
                for j in range(3):
                    if order[i][j] == entry:
                        term = value * spectrum[j]
                        totals[i] = term if totals[i] is None else totals[i] + term
            if edge:
                value = raw * weights[4] + raw_turned * weights[5]
                for i in range(3):
                    for j in range(3):
                        if order[i][j] == entry:
                            totals[i] = totals[i] + value * spectrum[3 + j]
        columns = [
            stacked_parts(jnp.concatenate([total, turn(total) * signs], axis=0)) for total in totals
        ]
        mixed = product(inverse_ref[...], jnp.concatenate(columns, axis=1))
        for component in range(3):
            value = mixed[:, component * depth : (component + 1) * depth]
            for index, out_ref in enumerate(out_refs):
                for far, place in enumerate(places(component, row)):
                    begin = (index * outer + far) * planes
                    out_ref[place : place + planes, :] = value[begin : begin + planes]


def gathered_columns(component, in_refs, mask_ref, table_ref, planes):
    part = mask_ref.shape[1] // len(in_refs)
    columns = []
    for plane in range(planes):
        start = component * part * planes + plane
        value = jnp.concatenate(
            [ref[pl.ds(start, part, stride=planes), :] for ref in in_refs], axis=0
        )
        turned = turn(value)
        top = value * mask_ref[0] + turned * mask_ref[1]
        bottom = value * mask_ref[2] + turned * mask_ref[3]
        columns.append(stacked_parts(jnp.concatenate([top, bottom], axis=0)))
    return product(table_ref[...], jnp.concatenate(columns, axis=1))


def backward_kernel(table_ref, mask_ref, *refs):
    in_refs, out_ref = refs[:-1], refs[-1]
    _, planes, _, depth = out_ref.shape
    for component in range(3):
        mixed = gathered_columns(component, in_refs, mask_ref, table_ref, planes)
        for plane in range(planes):
            out_ref[component, plane] = mixed[:, plane * depth : (plane + 1) * depth]


def cross_parts(left, right):
    return [
        left[1] * right[2] - left[2] * right[1],
        left[2] * right[0] - left[0] * right[2],
        left[0] * right[1] - left[1] * right[0],
    ]


def edge_planes(field_ref, bond_ref, first_ref, carried_ref):
    bond = bond_ref[0, 0].astype(jnp.float32)
    for component in range(3):
        first_ref[component] = field_ref[component, 0]
        carried_ref[component] = bond * field_ref[component, field_ref.shape[1] - 1]


def advance_kernel(edges, *refs):
    refs, (out_ref, *edge_refs, dipole_ref) = refs[: -2 - 2 * edges], refs[-2 - 2 * edges :]
    in_refs, refs = refs[:-7], refs[-7:]
    table_ref, mask_ref, depth_ref, partial_ref, local_ref, field_ref, bond_ref = refs
    _, planes, width, depth = out_ref.shape
    for component in range(3):
        mixed = gathered_columns(component, in_refs, mask_ref, table_ref, planes)
        lines = jnp.concatenate(
            [
                mixed[:, plane * depth : (plane + 1) * depth] + partial_ref[component, plane]
                for plane in range(planes)
            ],
            axis=0,
        )
        high, low = split(lines)
        field = product(jnp.concatenate([high, high, low], axis=1), depth_ref[...])
        dipole_ref[component] = field.reshape(planes, width, depth)
    for plane in range(planes):
        moment = [field_ref[component, plane] for component in range(3)]
        effective = [local_ref[c, plane] + dipole_ref[c, plane] for c in range(3)]
        torque = cross_parts(moment, effective)
        twice = cross_parts(moment, torque)
        stepped = [moment[c] - TIME_STEP * (torque[c] + DAMPING * twice[c]) for c in range(3)]
        scale = lax.rsqrt(
            stepped[0] * stepped[0] + stepped[1] * stepped[1] + stepped[2] * stepped[2]
        )
        for component in range(3):
            out_ref[component, plane] = stepped[component] * scale
    if edges:
        edge_planes(out_ref, bond_ref, *edge_refs)


def local_kernel(
    step, scale_ref, field_ref, above_ref, below_ref, bond_ref, noise_ref, out_ref, held_ref, sem
):
    _, planes, width, depth = out_ref.shape
    copy = pltpu.make_async_copy(noise_ref.at[step], held_ref, sem)
    copy.start()
    copy.wait()
    scale = scale_ref[step : step + 1, :]
    for plane in range(planes):
        bonds = [bond_ref[d, plane].astype(jnp.float32) for d in range(3)]
        if plane:
            bond_before = bond_ref[0, plane - 1].astype(jnp.float32)
        for component in range(3):
            value = field_ref[component, plane]
            upper = field_ref[component, plane + 1] if plane + 1 < planes else above_ref[component]
            if plane:
                lower = bond_before * field_ref[component, plane - 1]
            else:
                lower = below_ref[component]
            total = bonds[0] * upper + lower
            total = total + bonds[1] * pltpu.roll(value, width - 1, 0)
            total = total + pltpu.roll(bonds[1] * value, 1, 0)
            total = total + bonds[2] * pltpu.roll(value, depth - 1, 1)
            total = total + pltpu.roll(bonds[2] * value, 1, 1)
            out_ref[component, plane] = total + scale * held_ref[component, plane].astype(
                jnp.float32
            )


def call(
    kernel, outs, operands, scratch=(), specs=None, out_specs=None, lead=(), before=(), after=(), mib=16
):
    specs = {} if specs is None else specs
    out_specs = {} if out_specs is None else out_specs
    whole = pl.BlockSpec(memory_space=pltpu.VMEM)
    unread = pl.BlockSpec(memory_space=pl.ANY)
    count = len(operands)
    order = [*lead, *(i for i in range(count) if i not in lead)]

    def body(*refs):
        refs = refs[len(before) :]
        taken = dict(zip(order, refs))
        kernel(*(taken[i] for i in range(count)), *refs[count + len(after) :])

    return pl.pallas_call(
        body,
        out_shape=list(outs),
        in_specs=[unread] * len(before)
        + [specs.get(i, whole) for i in order]
        + [unread] * len(after),
        out_specs=[out_specs.get(i, whole) for i in range(len(outs))],
        scratch_shapes=list(scratch),
        cost_estimate=pl.CostEstimate(flops=1, bytes_accessed=1, transcendentals=0),
        compiler_params=pltpu.CompilerParams(vmem_limit_bytes=mib * 1024 * 1024),
    )(*before, *(operands[i] for i in order), *after)


def shape_of(*shape, dtype=jnp.float32):
    return jax.ShapeDtypeStruct(shape, dtype)


def log2(size):
    return size.bit_length() - 1


class Route:
    def __init__(self, start, rows, first, second):
        self.start, self.rows, self.first, self.second = start, rows, first, second

    def distance(self, index, second_leads):
        lead, last = (self.second, self.first) if second_leads else (self.first, self.second)
        return (index >> log2(last[0])) * lead[1] + (index & (last[0] - 1)) * last[1]

    def waves(self, me, index, row_block):
        block = me ^ self.distance(index >> log2(self.rows), False)
        return block * row_block + self.start + (index & (self.rows - 1))

    def cells(self, me, index, planes):
        block = me ^ self.distance(index >> log2(planes), True)
        return block * planes + (index & (planes - 1))


def angles(left, right, length):
    angle = (2.0 * math.pi / length) * ((left * right) & (length - 1)).astype(jnp.float32)
    return jnp.cos(angle), jnp.sin(angle)


def table_parts(table):
    high, low = split(table)
    return jnp.concatenate([high, low, high], axis=1)


def iota(shape, axis):
    return lax.broadcasted_iota(jnp.int32, shape, axis)


def forward_tables(routes, row_block, me_ref, *out_refs):
    me = me_ref[0]
    for route, table_ref, mask_ref in zip(routes, out_refs[0::2], out_refs[1::2]):
        _, count, depth = mask_ref.shape
        width = table_ref.shape[1] // 6
        wave = route.waves(me, iota((count, width), 0), row_block)
        cosine, sine = angles(wave, iota((count, width), 1), width)
        table_ref[...] = table_parts(jnp.concatenate([cosine, sine], axis=1))
        wave = route.waves(me, iota((count, depth), 0), row_block)
        lane = iota((count, depth), 1)
        below = (wave > 0) & (wave < width // 2) & (lane == depth // 2)
        above = (wave > width // 2) & ((lane == 0) | (lane == depth // 2))
        mask_ref[0] = jnp.where(below, 1.0, 0.0)
        mask_ref[1] = jnp.where(above, 1.0, 0.0)


def other_tables(routes, row_block, planes, me_ref, temps_ref, order_ref, accept_ref, *out_refs):
    labels_ref, scale_ref, weight_ref, *out_refs = out_refs
    me = me_ref[0]
    for pair in range(order_ref.shape[0] // 2):
        left, right = order_ref[2 * pair], order_ref[2 * pair + 1]
        swapped = (accept_ref[left] == 1) & (accept_ref[right] == 1)
        labels_ref[left] = jnp.where(swapped, right, left)
        labels_ref[right] = jnp.where(swapped, left, right)
    for step, slot in enumerate((me_ref[1], labels_ref[me_ref[1]])):
        picked = jnp.full((1, scale_ref.shape[1]), temps_ref[slot], jnp.float32)
        scale_ref[step : step + 1, :] = jnp.sqrt(2.0 * DAMPING * picked / TIME_STEP)
    depth = weight_ref.shape[1]
    half = depth // 2
    for index, route in enumerate(routes):
        into_ref, out_ref, table_ref, mask_ref = out_refs[4 * index : 4 * index + 4]
        cells = into_ref.shape[0]
        shape = (cells, cells)
        cosine, sine = angles(route.cells(me, iota(shape, 1), planes), iota(shape, 0), cells)
        into_ref[...] = table_parts(jnp.concatenate([cosine, sine], axis=1))
        cosine, sine = angles(route.cells(me, iota(shape, 0), planes), iota(shape, 1), cells)
        out_ref[...] = table_parts(jnp.concatenate([-cosine, sine], axis=1) / cells)
        count = mask_ref.shape[1]
        width = table_ref.shape[0]
        shape = (width, count)
        wave = route.waves(me, iota(shape, 1), row_block)
        cosine, sine = angles(wave, iota(shape, 0), width)
        table_ref[...] = table_parts(jnp.concatenate([cosine, sine], axis=1) / width)
        shape = (count, depth)
        wave = route.waves(me, iota(shape, 0), row_block)
        lane = iota(shape, 1)
        first, last = lane == 0, lane == half
        pair = first | last
        below = (wave > 0) & (wave < width // 2) & first
        above = (wave > width // 2) & last
        ends = (wave == 0) | (wave == width // 2)
        sign = jnp.where(lane < half, -1.0, 1.0)
        mask_ref[0] = jnp.where(pair, jnp.where(ends, 1.0, jnp.where(below, 2.0, 0.0)), 1.0)
        mask_ref[1] = jnp.where(above, 2.0, 0.0)
        mask_ref[2] = jnp.where(above, -2.0, 0.0)
        mask_ref[3] = jnp.where(pair, jnp.where(below, -2.0, 0.0), sign)
    blocks = width // row_block
    ends = jnp.where((me & (blocks // 2 - 1)) == 0, 1.0, 0.0)
    upper = jnp.where(me >= blocks // 2, 1.0, 0.0)
    lane = iota((1, depth), 1)
    first, last = lane == 0, lane == half
    direct = jnp.where(first, 1.0 - upper, jnp.where(last, upper, jnp.where(lane < half, 1.0, 0.0)))
    both = jnp.where(first | last, 0.5 * ends, 0.0)
    keep = jnp.where(first | last, 1.0 - ends, 1.0)
    flip = jnp.where(first, both, -both)
    kinds = [
        direct,
        1.0 - direct,
        direct * keep + both,
        (1.0 - direct) * keep + both,
        flip,
        -flip,
    ]
    for index, kind in enumerate(kinds):
        weight_ref[index : index + 1, :] = kind


def repack_forward(count, unit, *refs):
    in_refs, out_refs = refs[:count], refs[count:]
    outs = len(out_refs)
    for out_index, out_ref in enumerate(out_refs):
        for in_index, in_ref in enumerate(in_refs):
            for component in range(3):
                place, start = (in_index * 3 + component) * unit, (component * outs + out_index) * unit
                out_ref[place : place + unit, :] = in_ref[start : start + unit, :]


def repack_backward(count, unit, *refs):
    in_refs, out_refs = refs[:count], refs[count:]
    for out_index, out_ref in enumerate(out_refs):
        for in_index, in_ref in enumerate(in_refs):
            for component in range(3):
                place, start = (component * count + in_index) * unit, (out_index * 3 + component) * unit
                out_ref[place : place + unit, :] = in_ref[start : start + unit, :]


def depth_tables(depth):
    half = depth // 2
    angle = 2.0 * np.pi / depth * np.outer(np.arange(depth), np.arange(half)) % (2.0 * np.pi)
    middle = np.where(np.arange(depth) % 2 == 0, 1.0, -1.0)[:, None]
    into = np.concatenate([np.cos(angle), middle, -np.sin(angle[:, 1:])], axis=1)
    lane = np.arange(depth)
    out_of = (into * np.where(lane % half == 0, 1.0, 2.0) / depth).T
    tables = []
    for table in (into, out_of):
        high = table.astype(jnp.bfloat16)
        low = (table - high.astype(np.float64)).astype(jnp.bfloat16)
        tables.append(jnp.asarray(np.concatenate([high, low, high], axis=0)))
    return tables


def on_device(moments, couplings, noise, kernel, temps, order, accept):
    planes, width, depth = moments.shape[2:]
    row_block = kernel.shape[2]
    count = lax.axis_size("slab") * lax.axis_size("pen")
    if planes % 8 or row_block % 8 or depth % 128 or count & (count - 1) or moments.shape[0] > 1:
        return plain_on_device(moments, couplings, noise, kernel, temps, order, accept)
    near = (1 << (log2(count) // 2), 1)
    far = (count // near[0], near[0])
    rows = row_block // 2
    routes = [Route(0, rows, far, near), Route(rows, rows, near, far)]
    me = jnp.stack([lax.axis_index(AXES), lax.axis_index("temp")]).astype(jnp.int32)
    into_depth, out_of_depth = depth_tables(depth)
    lines = count * rows
    field = moments[0]
    whole = shape_of(*field.shape)
    plane_shape = shape_of(3, width, depth)
    forward = call(
        functools.partial(forward_tables, routes, row_block),
        [shape_of(lines, 6 * width, dtype=jnp.bfloat16), shape_of(2, lines, depth)] * 2,
        [me],
        specs={0: SCALARS},
    )
    square = shape_of(width, 6 * width, dtype=jnp.bfloat16)
    labels, scales, weights, *others = call(
        functools.partial(other_tables, routes, row_block, planes),
        [shape_of(*order.shape, dtype=jnp.int32), shape_of(2, depth), shape_of(6, depth)]
        + [square, square, shape_of(width, 6 * lines, dtype=jnp.bfloat16), shape_of(4, lines, depth)]
        * 2,
        [me, temps, order, accept],
        specs={i: SCALARS for i in range(4)},
        out_specs={0: SCALARS},
    )
    others = [others[:4], others[4:]]
    kernel_rows = kernel.reshape(6, width * row_block, depth)
    noise = noise[:, 0]
    unread = pl.BlockSpec(memory_space=pl.ANY)

    def exchange(blocks, stage):
        size, stride = stage
        moved = list(blocks)
        for index in range(1, size):
            distance = index * stride
            moved[index] = lax.ppermute(
                blocks[index], AXES, [(i, i ^ distance) for i in range(count)]
            )
        return moved

    unit = rows * planes

    def waits(stage, place=0):
        order = FAR_ORDER if stage is far else NEAR_ORDER
        return [place + i for i in (order if len(order) == stage[0] else range(stage[0]))]

    def blocks_of(stage):
        size = 3 * (count // stage[0]) * unit
        extras = FAR_EXTRA if stage is far else NEAR_EXTRA
        return [shape_of(size + (extras[i] if i < len(extras) else 0), depth) for i in range(stage[0])]

    def forward_part(field):
        groups = [route.first[0] for route in routes]
        blocks = call(
            functools.partial(forward_kernel, groups),
            blocks_of(routes[0].first) + blocks_of(routes[1].first),
            [field, into_depth, *forward],
        )
        return blocks[: groups[0]], blocks[groups[0] :]

    def forward_repack(chunk, blocks, **order):
        first, second = routes[chunk].first, routes[chunk].second
        kernel_of = functools.partial(repack_forward, first[0], unit)
        return call(kernel_of, blocks_of(second), blocks, lead=waits(first), **order)

    def middle_part(chunk, blocks, **order):
        second = routes[chunk].second
        return call(
            functools.partial(middle_kernel, routes[chunk].start, rows, second[0], planes),
            blocks_of(second),
            [kernel_rows, weights, *others[chunk][:2]] + list(blocks),
            lead=waits(second, 4),
            **order,
        )

    def backward_repack(chunk, blocks, **order):
        first, second = routes[chunk].first, routes[chunk].second
        kernel_of = functools.partial(repack_backward, second[0], unit)
        return call(kernel_of, blocks_of(first), blocks, lead=waits(second), **order)

    first_plane = field[:, 0]
    carried = couplings[0, -1].astype(jnp.float32) * field[:, -1]
    for step in range(2):
        a_out, b_out = forward_part(field)
        a_far = exchange(a_out, far)
        b_near = exchange(b_out, near)
        b_packed = forward_repack(1, b_near)
        a_packed = forward_repack(0, a_far)
        b_far = exchange(b_packed, far)
        a_near = exchange(a_packed, near)
        a_mid = middle_part(0, a_near)
        b_mid = middle_part(1, b_far, before=a_mid[:1])
        above = shifted(first_plane, AXES, -1)
        below = shifted(carried, AXES, 1)
        b_back = exchange(b_mid, far)
        a_back = exchange(a_mid, near)
        a_home = backward_repack(0, a_back, after=[above, below])
        b_home = backward_repack(1, b_back, before=a_home[:1])
        a_done = exchange(a_home, far)
        b_done = exchange(b_home, near)
        (local,) = call(
            functools.partial(local_kernel, step),
            [whole],
            [scales, field, above, below, couplings, noise],
            scratch=[pltpu.VMEM(field.shape, noise.dtype), pltpu.SemaphoreType.DMA(())],
            specs={5: unread},
            before=a_home[:1],
        )
        (sums,) = call(
            backward_kernel,
            [whole],
            [others[1][2], others[1][3]] + b_done,
            lead=waits(near, 2),
            after=[local],
        )
        edges = step == 0
        field, *planes_out = call(
            functools.partial(advance_kernel, edges),
            [whole] + [plane_shape] * 2 * edges,
            a_done
            + [others[0][2], others[0][3], out_of_depth, sums, local, field, couplings[:1, -1:]],
            lead=waits(far),
            scratch=[pltpu.VMEM(whole.shape, jnp.float32)],
        )
        if edges:
            first_plane, carried = planes_out
    return (field[None], labels)


def solution(mesh):
    return jax.shard_map(
        on_device,
        mesh=mesh,
        in_specs=(
            P(("groups", "temp"), None, ("slab", "pen"), None, None),
            P("groups", ("slab", "pen"), None, None),
            P(None, ("groups", "temp"), None, ("slab", "pen"), None, None),
            P(None, None, ("slab", "pen"), None),
            P(),
            P("groups"),
            P("groups"),
        ),
        out_specs=(P(("groups", "temp"), None, ("slab", "pen"), None, None), P("groups")),
        check_vma=False,
    )
```

```python
import functools
import math

import jax
import jax.numpy as jnp
import numpy as np
from jax import lax
from jax.experimental import pallas as pl
from jax.experimental.pallas import tpu as pltpu
from jax.sharding import PartitionSpec as P

TIME_STEP = 0.1
DAMPING = 0.5
AXES = ("slab", "pen")
FAR_ORDER = (3, 1, 2, 0)
NEAR_ORDER = (2, 3, 1, 0)
FAR_EXTRA = (0, 1, 1, 1)
NEAR_EXTRA = (0, 0, 0, 0)
SCALARS = pl.BlockSpec(memory_space=pltpu.SMEM)


def shifted(block, axis, distance):
    devices = range(lax.axis_size(axis))
    route = [((i - distance) % len(devices), i) for i in devices]
    return lax.ppermute(block, axis, route)


def cross(left, right, axis):
    left_parts = [lax.index_in_dim(left, component, axis, keepdims=False) for component in range(3)]
    right_parts = [
        lax.index_in_dim(right, component, axis, keepdims=False) for component in range(3)
    ]
    result = [
        left_parts[1] * right_parts[2] - left_parts[2] * right_parts[1],
        left_parts[2] * right_parts[0] - left_parts[0] * right_parts[2],
        left_parts[0] * right_parts[1] - left_parts[1] * right_parts[0],
    ]
    return jnp.stack(result, axis=axis)


def pair_labels(order, accept):
    slot_index = jnp.arange(order.shape[0], dtype=jnp.int32)
    position = jnp.sum(
        jnp.where(order[None, :] == slot_index[:, None], slot_index[None, :], 0), axis=1
    )
    mate_position = position + 1 - 2 * (position % 2)
    partner = jnp.sum(
        jnp.where(slot_index[None, :] == mate_position[:, None], order[None, :], 0), axis=1
    )
    partner_flag = jnp.sum(
        jnp.where(slot_index[None, :] == partner[:, None], accept[None, :], 0), axis=1
    )
    accepted = accept * partner_flag
    return jnp.where(accepted == 1, partner, slot_index)


def slot_sigma(labels, temps):
    slot_index = jnp.arange(temps.shape[0], dtype=jnp.int32)
    picked = jnp.sum(
        jnp.where(
            labels[:, None] == slot_index[None, :], temps[None, :], jnp.zeros_like(temps)[None, :]
        ),
        axis=1,
    )
    return jnp.sqrt(2.0 * DAMPING * picked / TIME_STEP)


def angle_tables(length):
    positions = jnp.arange(length, dtype=jnp.int32)
    product = positions[:, None] * positions[None, :] % length
    angles = 2.0 * math.pi / length * product.astype(jnp.float32)
    return (jnp.cos(angles), jnp.sin(angles))


def twist(packed, cosine_table, sine_table, pattern, orientation):
    cosine_part = jnp.einsum(pattern, packed, cosine_table, precision=lax.Precision.HIGHEST)
    sine_part = jnp.einsum(pattern, packed, sine_table, precision=lax.Precision.HIGHEST)
    middle = packed.shape[-1] // 2
    turned = jnp.concatenate([sine_part[..., middle:], -sine_part[..., :middle]], axis=-1)
    return cosine_part + orientation * turned


def pair_twist(stacked, cosine_table, sine_table, pattern, orientation):
    real_part = stacked[:, 0]
    imag_part = stacked[:, 1]
    real_cos = jnp.einsum(pattern, real_part, cosine_table, precision=lax.Precision.HIGHEST)
    real_sin = jnp.einsum(pattern, real_part, sine_table, precision=lax.Precision.HIGHEST)
    imag_cos = jnp.einsum(pattern, imag_part, cosine_table, precision=lax.Precision.HIGHEST)
    imag_sin = jnp.einsum(pattern, imag_part, sine_table, precision=lax.Precision.HIGHEST)
    return jnp.stack([real_cos + orientation * imag_sin, imag_cos - orientation * real_sin], axis=1)


def apply_kernel(spectrum, widened, replicas):
    shaped = spectrum.reshape((replicas, 3) + spectrum.shape[1:])
    comp_one, comp_two, comp_three = (shaped[:, 0], shaped[:, 1], shaped[:, 2])
    result = [
        -(widened[0] * comp_one + widened[3] * comp_two + widened[4] * comp_three),
        -(widened[3] * comp_one + widened[1] * comp_two + widened[5] * comp_three),
        -(widened[4] * comp_one + widened[5] * comp_two + widened[2] * comp_three),
    ]
    return jnp.stack(result, axis=1).reshape(spectrum.shape)


def advance(moment_field, local_field, noise_scale, noise_step):
    effective = local_field + noise_scale[:, None, None, None, None] * noise_step.astype(
        jnp.float32
    )
    torque = cross(moment_field, effective, 1)
    stepped = moment_field - TIME_STEP * (torque + DAMPING * cross(moment_field, torque, 1))
    return stepped * lax.rsqrt(jnp.sum(stepped * stepped, axis=1, keepdims=True))


def neighbor_sum(moment_field, bond_field):
    coupling_first = bond_field[0]
    carried = coupling_first * moment_field
    above = shifted(moment_field[:, :, :1], ("slab", "pen"), -1)
    below = shifted(carried[:, :, -1:], ("slab", "pen"), 1)
    upward = jnp.concatenate([moment_field[:, :, 1:], above], axis=2)
    downward = jnp.concatenate([below, carried[:, :, :-1]], axis=2)
    summed = coupling_first * upward + downward
    for grid_axis in (1, 2):
        coupling = bond_field[grid_axis]
        summed = (
            summed
            + coupling * jnp.roll(moment_field, -1, grid_axis + 2)
            + jnp.roll(coupling * moment_field, 1, grid_axis + 2)
        )
    return summed


def plain_on_device(moments, couplings, noise, kernel, temps, order, accept):
    replicas = moments.shape[0]
    planes = moments.shape[2]
    grid_width = moments.shape[3]
    grid_depth = moments.shape[4]
    slab_count = lax.axis_size("slab")
    pen_count = lax.axis_size("pen")
    slices = slab_count * pen_count
    row_block = grid_width // slices
    channels = 3 * replicas
    low_count = grid_depth // 2
    cosine_depth, sine_depth = angle_tables(grid_depth)
    cosine_width, sine_width = angle_tables(grid_width)
    inverse_cosine = cosine_width / grid_width
    inverse_sine = sine_width / grid_width
    low_weights = jnp.where(jnp.arange(low_count) == 0, 1.0, 2.0).astype(jnp.float32)
    forward_lower = jnp.concatenate(
        [cosine_depth[:, :low_count], -sine_depth[:, :low_count]], axis=1
    )
    backward_lower = (
        jnp.concatenate(
            [
                low_weights[:, None] * cosine_depth[:low_count],
                -low_weights[:, None] * sine_depth[:low_count],
            ],
            axis=0,
        )
        / grid_depth
    )
    kernel_lower = jnp.concatenate([kernel[..., :low_count], kernel[..., :low_count]], axis=-1)
    edge_column = cosine_depth[:, low_count]
    edge_row = cosine_depth[low_count] / grid_depth
    edge_kernel = jnp.swapaxes(kernel[..., low_count], 1, 2)[:, None]
    bond_field = couplings.astype(jnp.float32)
    labels = pair_labels(order, accept)
    slot_index = jnp.arange(temps.shape[0], dtype=jnp.int32)
    offset = lax.axis_index("temp") * replicas
    own_slots = lax.dynamic_slice_in_dim(slot_index, offset, replicas)
    own_labels = lax.dynamic_slice_in_dim(labels, offset, replicas)
    scales = (slot_sigma(own_slots, temps), slot_sigma(own_labels, temps))
    moment_field = moments
    for step_index in range(2):
        flattened = moment_field.reshape(channels, planes, grid_width, grid_depth)
        dipole_lower_part = jnp.dot(flattened, forward_lower, precision=lax.Precision.HIGHEST)
        dipole_lower_part = twist(dipole_lower_part, cosine_width, sine_width, "cxyw,yk->cxkw", 1.0)
        edge = jnp.dot(flattened, edge_column, precision=lax.Precision.HIGHEST)
        edge_real = jnp.einsum("cxy,yk->ckx", edge, cosine_width, precision=lax.Precision.HIGHEST)
        edge_imag = -jnp.einsum("cxy,yk->ckx", edge, sine_width, precision=lax.Precision.HIGHEST)
        edge_edge_in = jnp.stack([edge_real, edge_imag], axis=1).reshape(
            channels, 2, slices, row_block, 1, planes
        )
        edge_edge_moved = lax.all_to_all(
            edge_edge_in, ("slab", "pen"), split_axis=2, concat_axis=4, tiled=True
        )
        dipole_edge_pair = edge_edge_moved.reshape(channels, 2, row_block, grid_width)
        lower_lower_in = dipole_lower_part.reshape(
            channels, 1, planes, slices, row_block, dipole_lower_part.shape[-1]
        )
        lower_lower_out = lax.all_to_all(
            lower_lower_in, ("slab", "pen"), split_axis=3, concat_axis=1, tiled=True
        )
        dipole_lower_part = lower_lower_out.reshape(
            channels, grid_width, row_block, dipole_lower_part.shape[-1]
        )
        dipole_edge_pair = pair_twist(
            dipole_edge_pair, cosine_width, sine_width, "cyx,xk->cyk", 1.0
        )
        dipole_edge_pair = apply_kernel(dipole_edge_pair, edge_kernel, replicas)
        dipole_edge_pair = pair_twist(
            dipole_edge_pair, inverse_cosine, inverse_sine, "cyx,xk->cyk", -1.0
        )
        dipole_lower_part = twist(dipole_lower_part, cosine_width, sine_width, "cxyw,xk->ckyw", 1.0)
        dipole_lower_part = apply_kernel(dipole_lower_part, kernel_lower, replicas)
        dipole_lower_part = twist(
            dipole_lower_part, inverse_cosine, inverse_sine, "cxyw,xk->ckyw", -1.0
        )
        edge_in = dipole_edge_pair.reshape(channels, 2, 1, row_block, slices, planes)
        edge_moved = lax.all_to_all(
            edge_in, ("slab", "pen"), split_axis=4, concat_axis=2, tiled=True
        )
        dipole_edge_pair = edge_moved.reshape(channels, 2, grid_width, planes)
        lower_in = dipole_lower_part.reshape(
            channels, slices, planes, 1, row_block, dipole_lower_part.shape[-1]
        )
        lower_out = lax.all_to_all(
            lower_in, ("slab", "pen"), split_axis=1, concat_axis=3, tiled=True
        )
        dipole_lower_part = lower_out.reshape(
            channels, planes, grid_width, dipole_lower_part.shape[-1]
        )
        dipole_lower_part = twist(
            dipole_lower_part, inverse_cosine, inverse_sine, "cxyw,yk->cxkw", -1.0
        )
        edge_field = jnp.einsum(
            "ckx,ky->cxy", dipole_edge_pair[:, 0], inverse_cosine, precision=lax.Precision.HIGHEST
        ) - jnp.einsum(
            "ckx,ky->cxy", dipole_edge_pair[:, 1], inverse_sine, precision=lax.Precision.HIGHEST
        )
        summed = (
            jnp.dot(dipole_lower_part, backward_lower, precision=lax.Precision.HIGHEST)
            + edge_field[..., None] * edge_row
        )
        local_field = neighbor_sum(moment_field, bond_field) + summed.reshape(moment_field.shape)
        moment_field = advance(moment_field, local_field, scales[step_index], noise[step_index])
    return (moment_field, labels)


def split(value):
    high = value.astype(jnp.bfloat16)
    low = (value - high.astype(jnp.float32)).astype(jnp.bfloat16)
    return high, low


def stacked_parts(value):
    high, low = split(value)
    return jnp.concatenate([high, high, low], axis=0)


def product(left, right):
    return jnp.dot(left, right, preferred_element_type=jnp.float32)


def turn(value):
    return pltpu.roll(value, value.shape[-1] // 2, value.ndim - 1)


def lane_index(shape):
    return lax.broadcasted_iota(jnp.int32, shape, len(shape) - 1)


def forward_kernel(groups, field_ref, depth_ref, *refs):
    table_refs, out_refs = refs[: 2 * len(groups)], refs[2 * len(groups) :]
    _, planes, width, depth = field_ref.shape
    half = depth // 2
    lane = lane_index((width, depth))
    signs = jnp.where(lane == 0, 0.0, jnp.where(lane < half, 1.0, -1.0))
    for component in range(3):
        high, low = split(field_ref[component].reshape(planes * width, depth))
        lines = product(jnp.concatenate([high, high, low], axis=1), depth_ref[...])
        extra = jnp.zeros((width, depth), jnp.float32)
        columns = []
        for plane in range(planes):
            line = lines[plane * width : (plane + 1) * width]
            turned = turn(line)
            moved = pltpu.roll(turned, plane, 1) if plane else turned
            extra = jnp.where(lane == plane, moved, extra)
            columns.append(stacked_parts(jnp.concatenate([line, turned * signs], axis=0)))
        columns.append(stacked_parts(jnp.concatenate([extra, -turn(extra)], axis=0)))
        columns = jnp.concatenate(columns, axis=1)
        outs = list(out_refs)
        for chunk, group in enumerate(groups):
            table_ref, mask_ref = table_refs[2 * chunk : 2 * chunk + 2]
            part = table_ref.shape[0] // group
            mixed = product(table_ref[...], columns)
            extra = mixed[:, planes * depth :]
            for plane in range(planes):
                value = mixed[:, plane * depth : (plane + 1) * depth]
                value = value - mask_ref[0] * pltpu.roll(extra, half - plane, 1)
                back = pltpu.roll(extra, depth - plane, 1) if plane else extra
                value = jnp.where(mask_ref[1] > 0.5, back, value)
                start = component * part * planes + plane
                for index, out_ref in enumerate(outs[:group]):
                    out_ref[pl.ds(start, part, stride=planes), :] = value[
                        index * part : (index + 1) * part
                    ]
            outs = outs[group:]


def middle_kernel(start, rows, inner, planes, kernel_ref, weight_ref, table_ref, inverse_ref, *refs):
    in_refs, out_refs = refs[:inner], refs[inner:]
    count, depth = table_ref.shape[0], weight_ref.shape[1]
    half = depth // 2
    outer = count // (inner * planes)
    row_block = kernel_ref.shape[1] // count

    def places(component, row):
        return [((far * 3 + component) * rows + row) * planes for far in range(outer)]

    lane = lane_index((count, depth))
    signs = jnp.where(lane < half, 1.0, -1.0)
    order = ((0, 3, 4), (3, 1, 5), (4, 5, 2))
    weights = [weight_ref[i : i + 1, :] for i in range(6)]
    for row in range(rows):
        spectrum, columns = [], []
        edge = start + row == 0
        for component in range(3):
            block = jnp.concatenate(
                [
                    ref[place : place + planes, :]
                    for ref in in_refs
                    for place in places(component, row)
                ],
                axis=0,
            )
            turned = turn(block)
            columns.append(stacked_parts(jnp.concatenate([block, turned * signs], axis=0)))
            if edge:
                mirror = jnp.concatenate([block * signs, -turned], axis=0)
                spectrum.append(stacked_parts(mirror))
        mixed = product(table_ref[...], jnp.concatenate(columns + spectrum, axis=1))
        spectrum = [mixed[:, i * depth : (i + 1) * depth] for i in range(mixed.shape[1] // depth)]
        totals = [None] * 3
        for entry in range(6):
            raw = kernel_ref[entry, pl.ds(start + row, count, stride=row_block), :]
            raw_turned = turn(raw)
            pick = 2 if edge else 0
            value = raw * weights[pick] + raw_turned * weights[pick + 1]
            for i in range(3):
                for j in range(3):
                    if order[i][j] == entry:
                        term = value * spectrum[j]
                        totals[i] = term if totals[i] is None else totals[i] + term
            if edge:
                value = raw * weights[4] + raw_turned * weights[5]
                for i in range(3):
                    for j in range(3):
                        if order[i][j] == entry:
                            totals[i] = totals[i] + value * spectrum[3 + j]
        columns = [
            stacked_parts(jnp.concatenate([total, turn(total) * signs], axis=0)) for total in totals
        ]
        mixed = product(inverse_ref[...], jnp.concatenate(columns, axis=1))
        for component in range(3):
            value = mixed[:, component * depth : (component + 1) * depth]
            for index, out_ref in enumerate(out_refs):
                for far, place in enumerate(places(component, row)):
                    begin = (index * outer + far) * planes
                    out_ref[place : place + planes, :] = value[begin : begin + planes]


def gathered_columns(component, in_refs, mask_ref, table_ref, planes):
    part = mask_ref.shape[1] // len(in_refs)
    columns = []
    for plane in range(planes):
        start = component * part * planes + plane
        value = jnp.concatenate(
            [ref[pl.ds(start, part, stride=planes), :] for ref in in_refs], axis=0
        )
        turned = turn(value)
        top = value * mask_ref[0] + turned * mask_ref[1]
        bottom = value * mask_ref[2] + turned * mask_ref[3]
        columns.append(stacked_parts(jnp.concatenate([top, bottom], axis=0)))
    return product(table_ref[...], jnp.concatenate(columns, axis=1))


def backward_kernel(table_ref, mask_ref, *refs):
    in_refs, out_ref = refs[:-1], refs[-1]
    _, planes, _, depth = out_ref.shape
    for component in range(3):
        mixed = gathered_columns(component, in_refs, mask_ref, table_ref, planes)
        for plane in range(planes):
            out_ref[component, plane] = mixed[:, plane * depth : (plane + 1) * depth]


def cross_parts(left, right):
    return [
        left[1] * right[2] - left[2] * right[1],
        left[2] * right[0] - left[0] * right[2],
        left[0] * right[1] - left[1] * right[0],
    ]


def edge_planes(field_ref, bond_ref, first_ref, carried_ref):
    bond = bond_ref[...].astype(jnp.float32)
    for component in range(3):
        first_ref[component] = field_ref[component, 0]
        carried_ref[component] = bond * field_ref[component, field_ref.shape[1] - 1]


def advance_kernel(edges, *refs):
    refs, (dipole_ref, *held) = refs[: -1 - 2 * edges], refs[-1 - 2 * edges :]
    refs, (out_ref, *edge_refs) = refs[: -1 - 2 * edges], refs[-1 - 2 * edges :]
    in_refs, refs = refs[:-7], refs[-7:]
    table_ref, mask_ref, depth_ref, partial_ref, local_ref, field_ref, bond_ref = refs
    if edges:
        bond = pltpu.make_async_copy(bond_ref.at[0, bond_ref.shape[1] - 1], *held)
        bond.start()
    _, planes, width, depth = out_ref.shape
    for component in range(3):
        mixed = gathered_columns(component, in_refs, mask_ref, table_ref, planes)
        lines = jnp.concatenate(
            [
                mixed[:, plane * depth : (plane + 1) * depth] + partial_ref[component, plane]
                for plane in range(planes)
            ],
            axis=0,
        )
        high, low = split(lines)
        field = product(jnp.concatenate([high, high, low], axis=1), depth_ref[...])
        dipole_ref[component] = field.reshape(planes, width, depth)
    for plane in range(planes):
        moment = [field_ref[component, plane] for component in range(3)]
        effective = [local_ref[c, plane] + dipole_ref[c, plane] for c in range(3)]
        torque = cross_parts(moment, effective)
        twice = cross_parts(moment, torque)
        stepped = [moment[c] - TIME_STEP * (torque[c] + DAMPING * twice[c]) for c in range(3)]
        scale = lax.rsqrt(
            stepped[0] * stepped[0] + stepped[1] * stepped[1] + stepped[2] * stepped[2]
        )
        for component in range(3):
            out_ref[component, plane] = stepped[component] * scale
    if edges:
        bond.wait()
        edge_planes(out_ref, held[0], *edge_refs)


def local_kernel(
    step, scale_ref, field_ref, above_ref, below_ref, bond_ref, noise_ref, out_ref, held_ref, sem
):
    _, planes, width, depth = out_ref.shape
    copy = pltpu.make_async_copy(noise_ref.at[step], held_ref, sem)
    copy.start()
    copy.wait()
    scale = scale_ref[step : step + 1, :]
    for plane in range(planes):
        bonds = [bond_ref[d, plane].astype(jnp.float32) for d in range(3)]
        if plane:
            bond_before = bond_ref[0, plane - 1].astype(jnp.float32)
        for component in range(3):
            value = field_ref[component, plane]
            upper = field_ref[component, plane + 1] if plane + 1 < planes else above_ref[component]
            if plane:
                lower = bond_before * field_ref[component, plane - 1]
            else:
                lower = below_ref[component]
            total = bonds[0] * upper + lower
            total = total + bonds[1] * pltpu.roll(value, width - 1, 0)
            total = total + pltpu.roll(bonds[1] * value, 1, 0)
            total = total + bonds[2] * pltpu.roll(value, depth - 1, 1)
            total = total + pltpu.roll(bonds[2] * value, 1, 1)
            out_ref[component, plane] = total + scale * held_ref[component, plane].astype(
                jnp.float32
            )


def call(
    kernel, outs, operands, scratch=(), specs=None, out_specs=None, lead=(), before=(), after=(), mib=16
):
    specs = {} if specs is None else specs
    out_specs = {} if out_specs is None else out_specs
    whole = pl.BlockSpec(memory_space=pltpu.VMEM)
    unread = pl.BlockSpec(memory_space=pl.ANY)
    count = len(operands)
    order = [*lead, *(i for i in range(count) if i not in lead)]

    def body(*refs):
        refs = refs[len(before) :]
        taken = dict(zip(order, refs))
        kernel(*(taken[i] for i in range(count)), *refs[count + len(after) :])

    return pl.pallas_call(
        body,
        out_shape=list(outs),
        in_specs=[unread] * len(before)
        + [specs.get(i, whole) for i in order]
        + [unread] * len(after),
        out_specs=[out_specs.get(i, whole) for i in range(len(outs))],
        scratch_shapes=list(scratch),
        cost_estimate=pl.CostEstimate(flops=1, bytes_accessed=1, transcendentals=0),
        compiler_params=pltpu.CompilerParams(vmem_limit_bytes=mib * 1024 * 1024),
    )(*before, *(operands[i] for i in order), *after)


def shape_of(*shape, dtype=jnp.float32):
    return jax.ShapeDtypeStruct(shape, dtype)


def log2(size):
    return size.bit_length() - 1


class Route:
    def __init__(self, start, rows, first, second):
        self.start, self.rows, self.first, self.second = start, rows, first, second

    def distance(self, index, second_leads):
        lead, last = (self.second, self.first) if second_leads else (self.first, self.second)
        return (index >> log2(last[0])) * lead[1] + (index & (last[0] - 1)) * last[1]

    def waves(self, me, index, row_block):
        block = me ^ self.distance(index >> log2(self.rows), False)
        return block * row_block + self.start + (index & (self.rows - 1))

    def cells(self, me, index, planes):
        block = me ^ self.distance(index >> log2(planes), True)
        return block * planes + (index & (planes - 1))


def angles(left, right, length):
    angle = (2.0 * math.pi / length) * ((left * right) & (length - 1)).astype(jnp.float32)
    return jnp.cos(angle), jnp.sin(angle)


def table_parts(table):
    high, low = split(table)
    return jnp.concatenate([high, low, high], axis=1)


def depth_table(cell, wave, depth):
    half = depth // 2
    cosine, sine = angles(cell, wave & (half - 1), depth)
    middle = (1 - 2 * (cell & 1)).astype(jnp.float32)
    return jnp.where(wave < half, cosine, jnp.where(wave == half, middle, -sine))


def row_parts(table):
    high, low = split(table)
    return jnp.concatenate([high, low, high], axis=0)


def iota(shape, axis):
    return lax.broadcasted_iota(jnp.int32, shape, axis)


def forward_tables(routes, row_block, me_ref, *out_refs):
    me = me_ref[0]
    for route, table_ref, mask_ref in zip(routes, out_refs[0::2], out_refs[1::2]):
        _, count, depth = mask_ref.shape
        width = table_ref.shape[1] // 6
        wave = route.waves(me, iota((count, width), 0), row_block)
        cosine, sine = angles(wave, iota((count, width), 1), width)
        table_ref[...] = table_parts(jnp.concatenate([cosine, sine], axis=1))
        wave = route.waves(me, iota((count, depth), 0), row_block)
        lane = iota((count, depth), 1)
        below = (wave > 0) & (wave < width // 2) & (lane == depth // 2)
        above = (wave > width // 2) & ((lane == 0) | (lane == depth // 2))
        mask_ref[0] = jnp.where(below, 1.0, 0.0)
        mask_ref[1] = jnp.where(above, 1.0, 0.0)


def first_kernel(routes, row_block, groups, me_ref, field_ref, *refs):
    blocks, (depth_ref, *table_refs, first_ref, last_ref) = refs[:-7], refs[-7:]
    depth = depth_ref.shape[1]
    shape = (depth, depth)
    depth_ref[...] = row_parts(depth_table(iota(shape, 0), iota(shape, 1), depth))
    forward_tables(routes, row_block, me_ref, *table_refs)
    forward_kernel(groups, field_ref, depth_ref, *table_refs, *blocks)
    for component in range(3):
        first_ref[component] = field_ref[component, 0]
        last_ref[component] = field_ref[component, field_ref.shape[1] - 1]


def other_tables(
    routes, row_block, planes, me_ref, temps_ref, order_ref, accept_ref, last_ref, bond_ref, *out_refs
):
    labels_ref, scale_ref, carried_ref, weight_ref, depth_ref, *out_refs = out_refs
    bond = bond_ref[0, planes - 1].astype(jnp.float32)
    for component in range(3):
        carried_ref[component] = bond * last_ref[component]
    me = me_ref[0]
    shape = (weight_ref.shape[1], weight_ref.shape[1])
    back = depth_table(iota(shape, 1), iota(shape, 0), shape[0])
    share = jnp.where((iota(shape, 0) & (shape[0] // 2 - 1)) == 0, 1.0, 2.0) / shape[0]
    depth_ref[...] = row_parts(back * share)
    for pair in range(order_ref.shape[0] // 2):
        left, right = order_ref[2 * pair], order_ref[2 * pair + 1]
        swapped = (accept_ref[left] == 1) & (accept_ref[right] == 1)
        labels_ref[left] = jnp.where(swapped, right, left)
        labels_ref[right] = jnp.where(swapped, left, right)
    for step, slot in enumerate((me_ref[1], labels_ref[me_ref[1]])):
        picked = jnp.full((1, scale_ref.shape[1]), temps_ref[slot], jnp.float32)
        scale_ref[step : step + 1, :] = jnp.sqrt(2.0 * DAMPING * picked / TIME_STEP)
    depth = weight_ref.shape[1]
    half = depth // 2
    for index, route in enumerate(routes):
        into_ref, out_ref, table_ref, mask_ref = out_refs[4 * index : 4 * index + 4]
        cells = into_ref.shape[0]
        shape = (cells, cells)
        cosine, sine = angles(route.cells(me, iota(shape, 1), planes), iota(shape, 0), cells)
        into_ref[...] = table_parts(jnp.concatenate([cosine, sine], axis=1))
        cosine, sine = angles(route.cells(me, iota(shape, 0), planes), iota(shape, 1), cells)
        out_ref[...] = table_parts(jnp.concatenate([-cosine, sine], axis=1) / cells)
        count = mask_ref.shape[1]
        width = table_ref.shape[0]
        shape = (width, count)
        wave = route.waves(me, iota(shape, 1), row_block)
        cosine, sine = angles(wave, iota(shape, 0), width)
        table_ref[...] = table_parts(jnp.concatenate([cosine, sine], axis=1) / width)
        shape = (count, depth)
        wave = route.waves(me, iota(shape, 0), row_block)
        lane = iota(shape, 1)
        first, last = lane == 0, lane == half
        pair = first | last
        below = (wave > 0) & (wave < width // 2) & first
        above = (wave > width // 2) & last
        ends = (wave == 0) | (wave == width // 2)
        sign = jnp.where(lane < half, -1.0, 1.0)
        mask_ref[0] = jnp.where(pair, jnp.where(ends, 1.0, jnp.where(below, 2.0, 0.0)), 1.0)
        mask_ref[1] = jnp.where(above, 2.0, 0.0)
        mask_ref[2] = jnp.where(above, -2.0, 0.0)
        mask_ref[3] = jnp.where(pair, jnp.where(below, -2.0, 0.0), sign)
    blocks = width // row_block
    ends = jnp.where((me & (blocks // 2 - 1)) == 0, 1.0, 0.0)
    upper = jnp.where(me >= blocks // 2, 1.0, 0.0)
    lane = iota((1, depth), 1)
    first, last = lane == 0, lane == half
    direct = jnp.where(first, 1.0 - upper, jnp.where(last, upper, jnp.where(lane < half, 1.0, 0.0)))
    both = jnp.where(first | last, 0.5 * ends, 0.0)
    keep = jnp.where(first | last, 1.0 - ends, 1.0)
    flip = jnp.where(first, both, -both)
    kinds = [
        direct,
        1.0 - direct,
        direct * keep + both,
        (1.0 - direct) * keep + both,
        flip,
        -flip,
    ]
    for index, kind in enumerate(kinds):
        weight_ref[index : index + 1, :] = kind


def repack_forward(count, unit, *refs):
    in_refs, out_refs = refs[:count], refs[count:]
    outs = len(out_refs)
    for out_index, out_ref in enumerate(out_refs):
        for in_index, in_ref in enumerate(in_refs):
            for component in range(3):
                place, start = (in_index * 3 + component) * unit, (component * outs + out_index) * unit
                out_ref[place : place + unit, :] = in_ref[start : start + unit, :]


def repack_backward(count, unit, *refs):
    in_refs, out_refs = refs[:count], refs[count:]
    for out_index, out_ref in enumerate(out_refs):
        for in_index, in_ref in enumerate(in_refs):
            for component in range(3):
                place, start = (component * count + in_index) * unit, (out_index * 3 + component) * unit
                out_ref[place : place + unit, :] = in_ref[start : start + unit, :]


def on_device(moments, couplings, noise, kernel, temps, order, accept):
    planes, width, depth = moments.shape[2:]
    row_block = kernel.shape[2]
    count = lax.axis_size("slab") * lax.axis_size("pen")
    if planes % 8 or row_block % 8 or depth % 128 or count & (count - 1) or moments.shape[0] > 1:
        return plain_on_device(moments, couplings, noise, kernel, temps, order, accept)
    near = (1 << (log2(count) // 2), 1)
    far = (count // near[0], near[0])
    rows = row_block // 2
    routes = [Route(0, rows, far, near), Route(rows, rows, near, far)]
    me = jnp.stack([lax.axis_index(AXES), lax.axis_index("temp")]).astype(jnp.int32)
    lines = count * rows
    field = moments[0]
    whole = shape_of(*field.shape)
    plane_shape = shape_of(3, width, depth)
    depth_shape = shape_of(3 * depth, depth, dtype=jnp.bfloat16)
    in_hbm = pl.BlockSpec(memory_space=pltpu.HBM)
    bond_held = pltpu.VMEM((width, depth), couplings.dtype)
    kernel_rows = kernel.reshape(6, width * row_block, depth)
    noise = noise[:, 0]

    def exchange(blocks, stage):
        size, stride = stage
        moved = list(blocks)
        for index in range(1, size):
            distance = index * stride
            moved[index] = lax.ppermute(
                blocks[index], AXES, [(i, i ^ distance) for i in range(count)]
            )
        return moved

    unit = rows * planes

    def waits(stage, place=0):
        order = FAR_ORDER if stage is far else NEAR_ORDER
        return [place + i for i in (order if len(order) == stage[0] else range(stage[0]))]

    def blocks_of(stage):
        size = 3 * (count // stage[0]) * unit
        extras = FAR_EXTRA if stage is far else NEAR_EXTRA
        return [shape_of(size + (extras[i] if i < len(extras) else 0), depth) for i in range(stage[0])]

    groups = [route.first[0] for route in routes]
    block_shapes = blocks_of(routes[0].first) + blocks_of(routes[1].first)

    def first_part():
        tables = [shape_of(lines, 6 * width, dtype=jnp.bfloat16), shape_of(2, lines, depth)] * 2
        outs = call(
            functools.partial(first_kernel, routes, row_block, groups),
            block_shapes + [depth_shape] + tables + [plane_shape] * 2,
            [me, field],
            specs={0: SCALARS},
        )
        return outs[:-7], outs[-7:-2], outs[-2:]

    def forward_part(field, tables):
        return call(functools.partial(forward_kernel, groups), block_shapes, [field, *tables])

    def forward_repack(chunk, blocks, **order):
        first, second = routes[chunk].first, routes[chunk].second
        kernel_of = functools.partial(repack_forward, first[0], unit)
        return call(kernel_of, blocks_of(second), blocks, lead=waits(first), **order)

    def middle_part(chunk, blocks, **order):
        second = routes[chunk].second
        return call(
            functools.partial(middle_kernel, routes[chunk].start, rows, second[0], planes),
            blocks_of(second),
            [kernel_rows, weights, *others[chunk][:2]] + list(blocks),
            lead=waits(second, 4),
            **order,
        )

    def backward_repack(chunk, blocks, **order):
        first, second = routes[chunk].first, routes[chunk].second
        kernel_of = functools.partial(repack_backward, second[0], unit)
        return call(kernel_of, blocks_of(first), blocks, lead=waits(second), **order)

    blocks, forward, (first_plane, last_plane) = first_part()
    square = shape_of(width, 6 * width, dtype=jnp.bfloat16)
    labels, scales, carried, weights, out_of_depth, *others = call(
        functools.partial(other_tables, routes, row_block, planes),
        [shape_of(*order.shape, dtype=jnp.int32), shape_of(2, depth), plane_shape]
        + [shape_of(6, depth), depth_shape]
        + [square, square, shape_of(width, 6 * lines, dtype=jnp.bfloat16), shape_of(4, lines, depth)]
        * 2,
        [me, temps, order, accept, last_plane, couplings],
        specs={i: SCALARS for i in range(4)},
        out_specs={0: SCALARS},
    )
    others = [others[:4], others[4:]]
    for step in range(2):
        if step:
            blocks = forward_part(field, forward)
        a_out, b_out = blocks[: groups[0]], blocks[groups[0] :]
        a_far = exchange(a_out, far)
        b_near = exchange(b_out, near)
        b_packed = forward_repack(1, b_near)
        a_packed = forward_repack(0, a_far)
        b_far = exchange(b_packed, far)
        a_near = exchange(a_packed, near)
        a_mid = middle_part(0, a_near)
        b_mid = middle_part(1, b_far, before=a_mid[:1])
        above = shifted(first_plane, AXES, -1)
        below = shifted(carried, AXES, 1)
        b_back = exchange(b_mid, far)
        a_back = exchange(a_mid, near)
        a_home = backward_repack(0, a_back, after=[above, below])
        b_home = backward_repack(1, b_back, before=a_home[:1])
        a_done = exchange(a_home, far)
        b_done = exchange(b_home, near)
        (local,) = call(
            functools.partial(local_kernel, step),
            [whole],
            [scales, field, above, below, couplings, noise],
            scratch=[pltpu.VMEM(field.shape, noise.dtype), pltpu.SemaphoreType.DMA(())],
            specs={5: in_hbm},
            before=a_home[:1],
        )
        (sums,) = call(
            backward_kernel,
            [whole],
            [others[1][2], others[1][3]] + b_done,
            lead=waits(near, 2),
            after=[local],
        )
        edges = step == 0
        field, *planes_out = call(
            functools.partial(advance_kernel, edges),
            [whole] + [plane_shape] * 2 * edges,
            a_done
            + [others[0][2], others[0][3], out_of_depth, sums, local, field, couplings],
            lead=waits(far),
            specs={len(a_done) + 6: in_hbm},
            scratch=[pltpu.VMEM(whole.shape, jnp.float32)]
            + [bond_held, pltpu.SemaphoreType.DMA(())] * edges,
        )
        if edges:
            first_plane, carried = planes_out
    return (field[None], labels)


def solution(mesh):
    return jax.shard_map(
        on_device,
        mesh=mesh,
        in_specs=(
            P(("groups", "temp"), None, ("slab", "pen"), None, None),
            P("groups", ("slab", "pen"), None, None),
            P(None, ("groups", "temp"), None, ("slab", "pen"), None, None),
            P(None, None, ("slab", "pen"), None),
            P(),
            P("groups"),
            P("groups"),
        ),
        out_specs=(P(("groups", "temp"), None, ("slab", "pen"), None, None), P("groups")),
        check_vma=False,
    )
```

```python
import functools
import math

import jax
import jax.numpy as jnp
import numpy as np
from jax import lax
from jax.experimental import pallas as pl
from jax.experimental.pallas import tpu as pltpu
from jax.sharding import PartitionSpec as P

TIME_STEP = 0.1
DAMPING = 0.5
AXES = ("slab", "pen")
FAR_ORDER = (3, 1, 2, 0)
NEAR_ORDER = (2, 3, 1, 0)
FAR_EXTRA = (0, 1, 1, 1)
NEAR_EXTRA = (0, 0, 0, 0)
SCALARS = pl.BlockSpec(memory_space=pltpu.SMEM)


def shifted(block, axis, distance):
    devices = range(lax.axis_size(axis))
    route = [((i - distance) % len(devices), i) for i in devices]
    return lax.ppermute(block, axis, route)


def cross(left, right, axis):
    left_parts = [lax.index_in_dim(left, component, axis, keepdims=False) for component in range(3)]
    right_parts = [
        lax.index_in_dim(right, component, axis, keepdims=False) for component in range(3)
    ]
    result = [
        left_parts[1] * right_parts[2] - left_parts[2] * right_parts[1],
        left_parts[2] * right_parts[0] - left_parts[0] * right_parts[2],
        left_parts[0] * right_parts[1] - left_parts[1] * right_parts[0],
    ]
    return jnp.stack(result, axis=axis)


def pair_labels(order, accept):
    slot_index = jnp.arange(order.shape[0], dtype=jnp.int32)
    position = jnp.sum(
        jnp.where(order[None, :] == slot_index[:, None], slot_index[None, :], 0), axis=1
    )
    mate_position = position + 1 - 2 * (position % 2)
    partner = jnp.sum(
        jnp.where(slot_index[None, :] == mate_position[:, None], order[None, :], 0), axis=1
    )
    partner_flag = jnp.sum(
        jnp.where(slot_index[None, :] == partner[:, None], accept[None, :], 0), axis=1
    )
    accepted = accept * partner_flag
    return jnp.where(accepted == 1, partner, slot_index)


def slot_sigma(labels, temps):
    slot_index = jnp.arange(temps.shape[0], dtype=jnp.int32)
    picked = jnp.sum(
        jnp.where(
            labels[:, None] == slot_index[None, :], temps[None, :], jnp.zeros_like(temps)[None, :]
        ),
        axis=1,
    )
    return jnp.sqrt(2.0 * DAMPING * picked / TIME_STEP)


def angle_tables(length):
    positions = jnp.arange(length, dtype=jnp.int32)
    product = positions[:, None] * positions[None, :] % length
    angles = 2.0 * math.pi / length * product.astype(jnp.float32)
    return (jnp.cos(angles), jnp.sin(angles))


def twist(packed, cosine_table, sine_table, pattern, orientation):
    cosine_part = jnp.einsum(pattern, packed, cosine_table, precision=lax.Precision.HIGHEST)
    sine_part = jnp.einsum(pattern, packed, sine_table, precision=lax.Precision.HIGHEST)
    middle = packed.shape[-1] // 2
    turned = jnp.concatenate([sine_part[..., middle:], -sine_part[..., :middle]], axis=-1)
    return cosine_part + orientation * turned


def pair_twist(stacked, cosine_table, sine_table, pattern, orientation):
    real_part = stacked[:, 0]
    imag_part = stacked[:, 1]
    real_cos = jnp.einsum(pattern, real_part, cosine_table, precision=lax.Precision.HIGHEST)
    real_sin = jnp.einsum(pattern, real_part, sine_table, precision=lax.Precision.HIGHEST)
    imag_cos = jnp.einsum(pattern, imag_part, cosine_table, precision=lax.Precision.HIGHEST)
    imag_sin = jnp.einsum(pattern, imag_part, sine_table, precision=lax.Precision.HIGHEST)
    return jnp.stack([real_cos + orientation * imag_sin, imag_cos - orientation * real_sin], axis=1)


def apply_kernel(spectrum, widened, replicas):
    shaped = spectrum.reshape((replicas, 3) + spectrum.shape[1:])
    comp_one, comp_two, comp_three = (shaped[:, 0], shaped[:, 1], shaped[:, 2])
    result = [
        -(widened[0] * comp_one + widened[3] * comp_two + widened[4] * comp_three),
        -(widened[3] * comp_one + widened[1] * comp_two + widened[5] * comp_three),
        -(widened[4] * comp_one + widened[5] * comp_two + widened[2] * comp_three),
    ]
    return jnp.stack(result, axis=1).reshape(spectrum.shape)


def advance(moment_field, local_field, noise_scale, noise_step):
    effective = local_field + noise_scale[:, None, None, None, None] * noise_step.astype(
        jnp.float32
    )
    torque = cross(moment_field, effective, 1)
    stepped = moment_field - TIME_STEP * (torque + DAMPING * cross(moment_field, torque, 1))
    return stepped * lax.rsqrt(jnp.sum(stepped * stepped, axis=1, keepdims=True))


def neighbor_sum(moment_field, bond_field):
    coupling_first = bond_field[0]
    carried = coupling_first * moment_field
    above = shifted(moment_field[:, :, :1], ("slab", "pen"), -1)
    below = shifted(carried[:, :, -1:], ("slab", "pen"), 1)
    upward = jnp.concatenate([moment_field[:, :, 1:], above], axis=2)
    downward = jnp.concatenate([below, carried[:, :, :-1]], axis=2)
    summed = coupling_first * upward + downward
    for grid_axis in (1, 2):
        coupling = bond_field[grid_axis]
        summed = (
            summed
            + coupling * jnp.roll(moment_field, -1, grid_axis + 2)
            + jnp.roll(coupling * moment_field, 1, grid_axis + 2)
        )
    return summed


def plain_on_device(moments, couplings, noise, kernel, temps, order, accept):
    replicas = moments.shape[0]
    planes = moments.shape[2]
    grid_width = moments.shape[3]
    grid_depth = moments.shape[4]
    slab_count = lax.axis_size("slab")
    pen_count = lax.axis_size("pen")
    slices = slab_count * pen_count
    row_block = grid_width // slices
    channels = 3 * replicas
    low_count = grid_depth // 2
    cosine_depth, sine_depth = angle_tables(grid_depth)
    cosine_width, sine_width = angle_tables(grid_width)
    inverse_cosine = cosine_width / grid_width
    inverse_sine = sine_width / grid_width
    low_weights = jnp.where(jnp.arange(low_count) == 0, 1.0, 2.0).astype(jnp.float32)
    forward_lower = jnp.concatenate(
        [cosine_depth[:, :low_count], -sine_depth[:, :low_count]], axis=1
    )
    backward_lower = (
        jnp.concatenate(
            [
                low_weights[:, None] * cosine_depth[:low_count],
                -low_weights[:, None] * sine_depth[:low_count],
            ],
            axis=0,
        )
        / grid_depth
    )
    kernel_lower = jnp.concatenate([kernel[..., :low_count], kernel[..., :low_count]], axis=-1)
    edge_column = cosine_depth[:, low_count]
    edge_row = cosine_depth[low_count] / grid_depth
    edge_kernel = jnp.swapaxes(kernel[..., low_count], 1, 2)[:, None]
    bond_field = couplings.astype(jnp.float32)
    labels = pair_labels(order, accept)
    slot_index = jnp.arange(temps.shape[0], dtype=jnp.int32)
    offset = lax.axis_index("temp") * replicas
    own_slots = lax.dynamic_slice_in_dim(slot_index, offset, replicas)
    own_labels = lax.dynamic_slice_in_dim(labels, offset, replicas)
    scales = (slot_sigma(own_slots, temps), slot_sigma(own_labels, temps))
    moment_field = moments
    for step_index in range(2):
        flattened = moment_field.reshape(channels, planes, grid_width, grid_depth)
        dipole_lower_part = jnp.dot(flattened, forward_lower, precision=lax.Precision.HIGHEST)
        dipole_lower_part = twist(dipole_lower_part, cosine_width, sine_width, "cxyw,yk->cxkw", 1.0)
        edge = jnp.dot(flattened, edge_column, precision=lax.Precision.HIGHEST)
        edge_real = jnp.einsum("cxy,yk->ckx", edge, cosine_width, precision=lax.Precision.HIGHEST)
        edge_imag = -jnp.einsum("cxy,yk->ckx", edge, sine_width, precision=lax.Precision.HIGHEST)
        edge_edge_in = jnp.stack([edge_real, edge_imag], axis=1).reshape(
            channels, 2, slices, row_block, 1, planes
        )
        edge_edge_moved = lax.all_to_all(
            edge_edge_in, ("slab", "pen"), split_axis=2, concat_axis=4, tiled=True
        )
        dipole_edge_pair = edge_edge_moved.reshape(channels, 2, row_block, grid_width)
        lower_lower_in = dipole_lower_part.reshape(
            channels, 1, planes, slices, row_block, dipole_lower_part.shape[-1]
        )
        lower_lower_out = lax.all_to_all(
            lower_lower_in, ("slab", "pen"), split_axis=3, concat_axis=1, tiled=True
        )
        dipole_lower_part = lower_lower_out.reshape(
            channels, grid_width, row_block, dipole_lower_part.shape[-1]
        )
        dipole_edge_pair = pair_twist(
            dipole_edge_pair, cosine_width, sine_width, "cyx,xk->cyk", 1.0
        )
        dipole_edge_pair = apply_kernel(dipole_edge_pair, edge_kernel, replicas)
        dipole_edge_pair = pair_twist(
            dipole_edge_pair, inverse_cosine, inverse_sine, "cyx,xk->cyk", -1.0
        )
        dipole_lower_part = twist(dipole_lower_part, cosine_width, sine_width, "cxyw,xk->ckyw", 1.0)
        dipole_lower_part = apply_kernel(dipole_lower_part, kernel_lower, replicas)
        dipole_lower_part = twist(
            dipole_lower_part, inverse_cosine, inverse_sine, "cxyw,xk->ckyw", -1.0
        )
        edge_in = dipole_edge_pair.reshape(channels, 2, 1, row_block, slices, planes)
        edge_moved = lax.all_to_all(
            edge_in, ("slab", "pen"), split_axis=4, concat_axis=2, tiled=True
        )
        dipole_edge_pair = edge_moved.reshape(channels, 2, grid_width, planes)
        lower_in = dipole_lower_part.reshape(
            channels, slices, planes, 1, row_block, dipole_lower_part.shape[-1]
        )
        lower_out = lax.all_to_all(
            lower_in, ("slab", "pen"), split_axis=1, concat_axis=3, tiled=True
        )
        dipole_lower_part = lower_out.reshape(
            channels, planes, grid_width, dipole_lower_part.shape[-1]
        )
        dipole_lower_part = twist(
            dipole_lower_part, inverse_cosine, inverse_sine, "cxyw,yk->cxkw", -1.0
        )
        edge_field = jnp.einsum(
            "ckx,ky->cxy", dipole_edge_pair[:, 0], inverse_cosine, precision=lax.Precision.HIGHEST
        ) - jnp.einsum(
            "ckx,ky->cxy", dipole_edge_pair[:, 1], inverse_sine, precision=lax.Precision.HIGHEST
        )
        summed = (
            jnp.dot(dipole_lower_part, backward_lower, precision=lax.Precision.HIGHEST)
            + edge_field[..., None] * edge_row
        )
        local_field = neighbor_sum(moment_field, bond_field) + summed.reshape(moment_field.shape)
        moment_field = advance(moment_field, local_field, scales[step_index], noise[step_index])
    return (moment_field, labels)


def split(value):
    high = value.astype(jnp.bfloat16)
    low = (value - high.astype(jnp.float32)).astype(jnp.bfloat16)
    return high, low


def stacked_parts(value):
    high, low = split(value)
    return jnp.concatenate([high, high, low], axis=0)


def product(left, right):
    return jnp.dot(left, right, preferred_element_type=jnp.float32)


def turn(value):
    return pltpu.roll(value, value.shape[-1] // 2, value.ndim - 1)


def lane_index(shape):
    return lax.broadcasted_iota(jnp.int32, shape, len(shape) - 1)


def forward_kernel(groups, field_ref, depth_ref, *refs):
    table_refs, out_refs = refs[: 2 * len(groups)], refs[2 * len(groups) :]
    _, planes, width, depth = field_ref.shape
    half = depth // 2
    lane = lane_index((width, depth))
    signs = jnp.where(lane == 0, 0.0, jnp.where(lane < half, 1.0, -1.0))
    for component in range(3):
        high, low = split(field_ref[component].reshape(planes * width, depth))
        lines = product(jnp.concatenate([high, high, low], axis=1), depth_ref[...])
        extra = jnp.zeros((width, depth), jnp.float32)
        columns = []
        for plane in range(planes):
            line = lines[plane * width : (plane + 1) * width]
            turned = turn(line)
            moved = pltpu.roll(turned, plane, 1) if plane else turned
            extra = jnp.where(lane == plane, moved, extra)
            columns.append(stacked_parts(jnp.concatenate([line, turned * signs], axis=0)))
        columns.append(stacked_parts(jnp.concatenate([extra, -turn(extra)], axis=0)))
        columns = jnp.concatenate(columns, axis=1)
        outs = list(out_refs)
        for chunk, group in enumerate(groups):
            table_ref, mask_ref = table_refs[2 * chunk : 2 * chunk + 2]
            part = table_ref.shape[0] // group
            mixed = product(table_ref[...], columns)
            extra = mixed[:, planes * depth :]
            for plane in range(planes):
                value = mixed[:, plane * depth : (plane + 1) * depth]
                value = value - mask_ref[0] * pltpu.roll(extra, half - plane, 1)
                back = pltpu.roll(extra, depth - plane, 1) if plane else extra
                value = jnp.where(mask_ref[1] > 0.5, back, value)
                start = component * part * planes + plane
                for index, out_ref in enumerate(outs[:group]):
                    out_ref[pl.ds(start, part, stride=planes), :] = value[
                        index * part : (index + 1) * part
                    ]
            outs = outs[group:]


def middle_kernel(start, rows, inner, planes, kernel_ref, weight_ref, table_ref, inverse_ref, *refs):
    in_refs, out_refs = refs[:inner], refs[inner:]
    count, depth = table_ref.shape[0], weight_ref.shape[1]
    half = depth // 2
    outer = count // (inner * planes)
    row_block = kernel_ref.shape[1] // count

    def places(component, row):
        return [((far * 3 + component) * rows + row) * planes for far in range(outer)]

    lane = lane_index((count, depth))
    signs = jnp.where(lane < half, 1.0, -1.0)
    order = ((0, 3, 4), (3, 1, 5), (4, 5, 2))
    weights = [weight_ref[i : i + 1, :] for i in range(6)]
    for row in range(rows):
        spectrum, columns = [], []
        edge = start + row == 0
        for component in range(3):
            block = jnp.concatenate(
                [
                    ref[place : place + planes, :]
                    for ref in in_refs
                    for place in places(component, row)
                ],
                axis=0,
            )
            turned = turn(block)
            columns.append(stacked_parts(jnp.concatenate([block, turned * signs], axis=0)))
            if edge:
                mirror = jnp.concatenate([block * signs, -turned], axis=0)
                spectrum.append(stacked_parts(mirror))
        mixed = product(table_ref[...], jnp.concatenate(columns + spectrum, axis=1))
        spectrum = [mixed[:, i * depth : (i + 1) * depth] for i in range(mixed.shape[1] // depth)]
        totals = [None] * 3
        for entry in range(6):
            raw = kernel_ref[entry, pl.ds(start + row, count, stride=row_block), :]
            raw_turned = turn(raw)
            pick = 2 if edge else 0
            value = raw * weights[pick] + raw_turned * weights[pick + 1]
            for i in range(3):
                for j in range(3):
                    if order[i][j] == entry:
                        term = value * spectrum[j]
                        totals[i] = term if totals[i] is None else totals[i] + term
            if edge:
                value = raw * weights[4] + raw_turned * weights[5]
                for i in range(3):
                    for j in range(3):
                        if order[i][j] == entry:
                            totals[i] = totals[i] + value * spectrum[3 + j]
        columns = [
            stacked_parts(jnp.concatenate([total, turn(total) * signs], axis=0)) for total in totals
        ]
        mixed = product(inverse_ref[...], jnp.concatenate(columns, axis=1))
        for component in range(3):
            value = mixed[:, component * depth : (component + 1) * depth]
            for index, out_ref in enumerate(out_refs):
                for far, place in enumerate(places(component, row)):
                    begin = (index * outer + far) * planes
                    out_ref[place : place + planes, :] = value[begin : begin + planes]


def gathered_columns(component, in_refs, mask_ref, table_ref, planes, chosen=None):
    part = mask_ref.shape[1] // len(in_refs)
    columns = []
    for plane in chosen or range(planes):
        start = component * part * planes + plane
        value = jnp.concatenate(
            [ref[pl.ds(start, part, stride=planes), :] for ref in in_refs], axis=0
        )
        turned = turn(value)
        top = value * mask_ref[0] + turned * mask_ref[1]
        bottom = value * mask_ref[2] + turned * mask_ref[3]
        columns.append(stacked_parts(jnp.concatenate([top, bottom], axis=0)))
    return product(table_ref[...], jnp.concatenate(columns, axis=1))


def backward_kernel(table_ref, mask_ref, *refs):
    in_refs, out_ref = refs[:-1], refs[-1]
    _, planes, _, depth = out_ref.shape
    for component in range(3):
        mixed = gathered_columns(component, in_refs, mask_ref, table_ref, planes)
        for plane in range(planes):
            out_ref[component, plane] = mixed[:, plane * depth : (plane + 1) * depth]


def cross_parts(left, right):
    return [
        left[1] * right[2] - left[2] * right[1],
        left[2] * right[0] - left[0] * right[2],
        left[0] * right[1] - left[1] * right[0],
    ]


def edge_planes(field_ref, bond_ref, first_ref, carried_ref):
    bond = bond_ref[...].astype(jnp.float32)
    for component in range(3):
        first_ref[component] = field_ref[component, 0]
        carried_ref[component] = bond * field_ref[component, field_ref.shape[1] - 1]


def advance_kernel(edges, *refs):
    scratch = 3 if edges else 2
    refs, (dipole_ref, *held) = refs[:-scratch], refs[-scratch:]
    refs, (out_ref, *edge_refs) = refs[: -1 - 2 * edges], refs[-1 - 2 * edges :]
    in_refs, refs = refs[:-7], refs[-7:]
    table_ref, mask_ref, depth_ref, partial_ref, local_ref, field_ref, bond_ref = refs
    if edges:
        bond = pltpu.make_async_copy(bond_ref.at[0, bond_ref.shape[1] - 1], *held)
        bond.start()
    _, planes, width, depth = out_ref.shape
    copies = []
    half = planes // 2
    for chosen in (range(half), range(half, planes)):
        for component in range(3):
            mixed = gathered_columns(component, in_refs, mask_ref, table_ref, planes, chosen)
            lines = jnp.concatenate(
                [
                    mixed[:, (plane - chosen[0]) * depth : (plane - chosen[0] + 1) * depth] + partial_ref[component, plane]
                    for plane in chosen
                ],
                axis=0,
            )
            high, low = split(lines)
            field = product(jnp.concatenate([high, high, low], axis=1), depth_ref[...])
            dipole_ref[component, chosen[0] : chosen[-1] + 1] = field.reshape(len(chosen), width, depth)
        for plane in chosen:
            moment = [field_ref[component, plane] for component in range(3)]
            effective = [local_ref[c, plane] + dipole_ref[c, plane] for c in range(3)]
            torque = cross_parts(moment, effective)
            twice = cross_parts(moment, torque)
            stepped = [moment[c] - TIME_STEP * (torque[c] + DAMPING * twice[c]) for c in range(3)]
            scale = lax.rsqrt(
                stepped[0] * stepped[0] + stepped[1] * stepped[1] + stepped[2] * stepped[2]
            )
            for component in range(3):
                target_ref = out_ref if edges else dipole_ref
                target_ref[component, plane] = stepped[component] * scale
            if not edges:
                copy = pltpu.make_async_copy(
                    dipole_ref.at[:, plane], out_ref.at[:, plane], held[0].at[plane]
                )
                copy.start()
                copies.append(copy)
    for copy in copies:
        copy.wait()
    if edges:
        bond.wait()
        edge_planes(out_ref, held[0], *edge_refs)


def local_kernel(
    step, scale_ref, field_ref, above_ref, below_ref, bond_ref, noise_ref, out_ref, held_ref, sem
):
    _, planes, width, depth = out_ref.shape
    copy = pltpu.make_async_copy(noise_ref.at[step], held_ref, sem)
    copy.start()
    copy.wait()
    scale = scale_ref[step : step + 1, :]
    for plane in range(planes):
        bonds = [bond_ref[d, plane].astype(jnp.float32) for d in range(3)]
        if plane:
            bond_before = bond_ref[0, plane - 1].astype(jnp.float32)
        for component in range(3):
            value = field_ref[component, plane]
            upper = field_ref[component, plane + 1] if plane + 1 < planes else above_ref[component]
            if plane:
                lower = bond_before * field_ref[component, plane - 1]
            else:
                lower = below_ref[component]
            total = bonds[0] * upper + lower
            total = total + bonds[1] * pltpu.roll(value, width - 1, 0)
            total = total + pltpu.roll(bonds[1] * value, 1, 0)
            total = total + bonds[2] * pltpu.roll(value, depth - 1, 1)
            total = total + pltpu.roll(bonds[2] * value, 1, 1)
            out_ref[component, plane] = total + scale * held_ref[component, plane].astype(
                jnp.float32
            )


def call(
    kernel, outs, operands, scratch=(), specs=None, out_specs=None, lead=(), before=(), after=(), mib=16
):
    specs = {} if specs is None else specs
    out_specs = {} if out_specs is None else out_specs
    whole = pl.BlockSpec(memory_space=pltpu.VMEM)
    unread = pl.BlockSpec(memory_space=pl.ANY)
    count = len(operands)
    order = [*lead, *(i for i in range(count) if i not in lead)]

    def body(*refs):
        refs = refs[len(before) :]
        taken = dict(zip(order, refs))
        kernel(*(taken[i] for i in range(count)), *refs[count + len(after) :])

    return pl.pallas_call(
        body,
        out_shape=list(outs),
        in_specs=[unread] * len(before)
        + [specs.get(i, whole) for i in order]
        + [unread] * len(after),
        out_specs=[out_specs.get(i, whole) for i in range(len(outs))],
        scratch_shapes=list(scratch),
        cost_estimate=pl.CostEstimate(flops=1, bytes_accessed=1, transcendentals=0),
        compiler_params=pltpu.CompilerParams(vmem_limit_bytes=mib * 1024 * 1024),
    )(*before, *(operands[i] for i in order), *after)


def shape_of(*shape, dtype=jnp.float32):
    return jax.ShapeDtypeStruct(shape, dtype)


def log2(size):
    return size.bit_length() - 1


class Route:
    def __init__(self, start, rows, first, second):
        self.start, self.rows, self.first, self.second = start, rows, first, second

    def distance(self, index, second_leads):
        lead, last = (self.second, self.first) if second_leads else (self.first, self.second)
        return (index >> log2(last[0])) * lead[1] + (index & (last[0] - 1)) * last[1]

    def waves(self, me, index, row_block):
        block = me ^ self.distance(index >> log2(self.rows), False)
        return block * row_block + self.start + (index & (self.rows - 1))

    def cells(self, me, index, planes):
        block = me ^ self.distance(index >> log2(planes), True)
        return block * planes + (index & (planes - 1))


def angles(left, right, length):
    angle = (2.0 * math.pi / length) * ((left * right) & (length - 1)).astype(jnp.float32)
    return jnp.cos(angle), jnp.sin(angle)


def table_parts(table):
    high, low = split(table)
    return jnp.concatenate([high, low, high], axis=1)


def depth_table(cell, wave, depth):
    half = depth // 2
    cosine, sine = angles(cell, wave & (half - 1), depth)
    middle = (1 - 2 * (cell & 1)).astype(jnp.float32)
    return jnp.where(wave < half, cosine, jnp.where(wave == half, middle, -sine))


def row_parts(table):
    high, low = split(table)
    return jnp.concatenate([high, low, high], axis=0)


def iota(shape, axis):
    return lax.broadcasted_iota(jnp.int32, shape, axis)


def forward_tables(routes, row_block, me_ref, *out_refs):
    me = me_ref[0]
    for route, table_ref, mask_ref in zip(routes, out_refs[0::2], out_refs[1::2]):
        _, count, depth = mask_ref.shape
        width = table_ref.shape[1] // 6
        wave = route.waves(me, iota((count, width), 0), row_block)
        cosine, sine = angles(wave, iota((count, width), 1), width)
        table_ref[...] = table_parts(jnp.concatenate([cosine, sine], axis=1))
        wave = route.waves(me, iota((count, depth), 0), row_block)
        lane = iota((count, depth), 1)
        below = (wave > 0) & (wave < width // 2) & (lane == depth // 2)
        above = (wave > width // 2) & ((lane == 0) | (lane == depth // 2))
        mask_ref[0] = jnp.where(below, 1.0, 0.0)
        mask_ref[1] = jnp.where(above, 1.0, 0.0)


def first_kernel(routes, row_block, groups, me_ref, field_ref, *refs):
    blocks, (depth_ref, *table_refs, first_ref, last_ref) = refs[:-7], refs[-7:]
    depth = depth_ref.shape[1]
    shape = (depth, depth)
    depth_ref[...] = row_parts(depth_table(iota(shape, 0), iota(shape, 1), depth))
    forward_tables(routes, row_block, me_ref, *table_refs)
    forward_kernel(groups, field_ref, depth_ref, *table_refs, *blocks)
    for component in range(3):
        first_ref[component] = field_ref[component, 0]
        last_ref[component] = field_ref[component, field_ref.shape[1] - 1]


def other_tables(
    routes, row_block, planes, me_ref, temps_ref, order_ref, accept_ref, last_ref, bond_ref, *out_refs
):
    labels_ref, scale_ref, carried_ref, weight_ref, depth_ref, *out_refs = out_refs
    bond = bond_ref[0, planes - 1].astype(jnp.float32)
    for component in range(3):
        carried_ref[component] = bond * last_ref[component]
    me = me_ref[0]
    shape = (weight_ref.shape[1], weight_ref.shape[1])
    back = depth_table(iota(shape, 1), iota(shape, 0), shape[0])
    share = jnp.where((iota(shape, 0) & (shape[0] // 2 - 1)) == 0, 1.0, 2.0) / shape[0]
    depth_ref[...] = row_parts(back * share)
    for pair in range(order_ref.shape[0] // 2):
        left, right = order_ref[2 * pair], order_ref[2 * pair + 1]
        swapped = (accept_ref[left] == 1) & (accept_ref[right] == 1)
        labels_ref[left] = jnp.where(swapped, right, left)
        labels_ref[right] = jnp.where(swapped, left, right)
    for step, slot in enumerate((me_ref[1], labels_ref[me_ref[1]])):
        picked = jnp.full((1, scale_ref.shape[1]), temps_ref[slot], jnp.float32)
        scale_ref[step : step + 1, :] = jnp.sqrt(2.0 * DAMPING * picked / TIME_STEP)
    depth = weight_ref.shape[1]
    half = depth // 2
    for index, route in enumerate(routes):
        into_ref, out_ref, table_ref, mask_ref = out_refs[4 * index : 4 * index + 4]
        cells = into_ref.shape[0]
        shape = (cells, cells)
        cosine, sine = angles(route.cells(me, iota(shape, 1), planes), iota(shape, 0), cells)
        into_ref[...] = table_parts(jnp.concatenate([cosine, sine], axis=1))
        cosine, sine = angles(route.cells(me, iota(shape, 0), planes), iota(shape, 1), cells)
        out_ref[...] = table_parts(jnp.concatenate([-cosine, sine], axis=1) / cells)
        count = mask_ref.shape[1]
        width = table_ref.shape[0]
        shape = (width, count)
        wave = route.waves(me, iota(shape, 1), row_block)
        cosine, sine = angles(wave, iota(shape, 0), width)
        table_ref[...] = table_parts(jnp.concatenate([cosine, sine], axis=1) / width)
        shape = (count, depth)
        wave = route.waves(me, iota(shape, 0), row_block)
        lane = iota(shape, 1)
        first, last = lane == 0, lane == half
        pair = first | last
        below = (wave > 0) & (wave < width // 2) & first
        above = (wave > width // 2) & last
        ends = (wave == 0) | (wave == width // 2)
        sign = jnp.where(lane < half, -1.0, 1.0)
        mask_ref[0] = jnp.where(pair, jnp.where(ends, 1.0, jnp.where(below, 2.0, 0.0)), 1.0)
        mask_ref[1] = jnp.where(above, 2.0, 0.0)
        mask_ref[2] = jnp.where(above, -2.0, 0.0)
        mask_ref[3] = jnp.where(pair, jnp.where(below, -2.0, 0.0), sign)
    blocks = width // row_block
    ends = jnp.where((me & (blocks // 2 - 1)) == 0, 1.0, 0.0)
    upper = jnp.where(me >= blocks // 2, 1.0, 0.0)
    lane = iota((1, depth), 1)
    first, last = lane == 0, lane == half
    direct = jnp.where(first, 1.0 - upper, jnp.where(last, upper, jnp.where(lane < half, 1.0, 0.0)))
    both = jnp.where(first | last, 0.5 * ends, 0.0)
    keep = jnp.where(first | last, 1.0 - ends, 1.0)
    flip = jnp.where(first, both, -both)
    kinds = [
        direct,
        1.0 - direct,
        direct * keep + both,
        (1.0 - direct) * keep + both,
        flip,
        -flip,
    ]
    for index, kind in enumerate(kinds):
        weight_ref[index : index + 1, :] = kind


def repack_forward(count, unit, *refs):
    in_refs, out_refs = refs[:count], refs[count:]
    outs = len(out_refs)
    for out_index, out_ref in enumerate(out_refs):
        for in_index, in_ref in enumerate(in_refs):
            for component in range(3):
                place, start = (in_index * 3 + component) * unit, (component * outs + out_index) * unit
                out_ref[place : place + unit, :] = in_ref[start : start + unit, :]


def repack_backward(count, unit, *refs):
    in_refs, out_refs = refs[:count], refs[count:]
    for out_index, out_ref in enumerate(out_refs):
        for in_index, in_ref in enumerate(in_refs):
            for component in range(3):
                place, start = (component * count + in_index) * unit, (out_index * 3 + component) * unit
                out_ref[place : place + unit, :] = in_ref[start : start + unit, :]


def on_device(moments, couplings, noise, kernel, temps, order, accept):
    planes, width, depth = moments.shape[2:]
    row_block = kernel.shape[2]
    count = lax.axis_size("slab") * lax.axis_size("pen")
    if planes % 8 or row_block % 8 or depth % 128 or count & (count - 1) or moments.shape[0] > 1:
        return plain_on_device(moments, couplings, noise, kernel, temps, order, accept)
    near = (1 << (log2(count) // 2), 1)
    far = (count // near[0], near[0])
    rows = row_block // 2
    routes = [Route(0, rows, far, near), Route(rows, rows, near, far)]
    me = jnp.stack([lax.axis_index(AXES), lax.axis_index("temp")]).astype(jnp.int32)
    lines = count * rows
    field = moments[0]
    whole = shape_of(*field.shape)
    plane_shape = shape_of(3, width, depth)
    depth_shape = shape_of(3 * depth, depth, dtype=jnp.bfloat16)
    in_hbm = pl.BlockSpec(memory_space=pltpu.HBM)
    bond_held = pltpu.VMEM((width, depth), couplings.dtype)
    kernel_rows = kernel.reshape(6, width * row_block, depth)
    noise = noise[:, 0]

    def exchange(blocks, stage):
        size, stride = stage
        moved = list(blocks)
        for index in range(1, size):
            distance = index * stride
            moved[index] = lax.ppermute(
                blocks[index], AXES, [(i, i ^ distance) for i in range(count)]
            )
        return moved

    unit = rows * planes

    def waits(stage, place=0):
        order = FAR_ORDER if stage is far else NEAR_ORDER
        return [place + i for i in (order if len(order) == stage[0] else range(stage[0]))]

    def blocks_of(stage):
        size = 3 * (count // stage[0]) * unit
        extras = FAR_EXTRA if stage is far else NEAR_EXTRA
        return [shape_of(size + (extras[i] if i < len(extras) else 0), depth) for i in range(stage[0])]

    groups = [route.first[0] for route in routes]
    block_shapes = blocks_of(routes[0].first) + blocks_of(routes[1].first)

    def first_part():
        tables = [shape_of(lines, 6 * width, dtype=jnp.bfloat16), shape_of(2, lines, depth)] * 2
        outs = call(
            functools.partial(first_kernel, routes, row_block, groups),
            block_shapes + [depth_shape] + tables + [plane_shape] * 2,
            [me, field],
            specs={0: SCALARS},
        )
        return outs[:-7], outs[-7:-2], outs[-2:]

    def forward_part(field, tables):
        return call(functools.partial(forward_kernel, groups), block_shapes, [field, *tables])

    def forward_repack(chunk, blocks, **order):
        first, second = routes[chunk].first, routes[chunk].second
        kernel_of = functools.partial(repack_forward, first[0], unit)
        return call(kernel_of, blocks_of(second), blocks, lead=waits(first), **order)

    def middle_part(chunk, blocks, **order):
        second = routes[chunk].second
        return call(
            functools.partial(middle_kernel, routes[chunk].start, rows, second[0], planes),
            blocks_of(second),
            [kernel_rows, weights, *others[chunk][:2]] + list(blocks),
            lead=waits(second, 4),
            **order,
        )

    def backward_repack(chunk, blocks, **order):
        first, second = routes[chunk].first, routes[chunk].second
        kernel_of = functools.partial(repack_backward, second[0], unit)
        return call(kernel_of, blocks_of(first), blocks, lead=waits(second), **order)

    blocks, forward, (first_plane, last_plane) = first_part()
    square = shape_of(width, 6 * width, dtype=jnp.bfloat16)
    labels, scales, carried, weights, out_of_depth, *others = call(
        functools.partial(other_tables, routes, row_block, planes),
        [shape_of(*order.shape, dtype=jnp.int32), shape_of(2, depth), plane_shape]
        + [shape_of(6, depth), depth_shape]
        + [square, square, shape_of(width, 6 * lines, dtype=jnp.bfloat16), shape_of(4, lines, depth)]
        * 2,
        [me, temps, order, accept, last_plane, couplings],
        specs={i: SCALARS for i in range(4)},
        out_specs={0: SCALARS},
    )
    others = [others[:4], others[4:]]
    for step in range(2):
        if step:
            blocks = forward_part(field, forward)
        a_out, b_out = blocks[: groups[0]], blocks[groups[0] :]
        a_far = exchange(a_out, far)
        b_near = exchange(b_out, near)
        b_packed = forward_repack(1, b_near)
        a_packed = forward_repack(0, a_far)
        b_far = exchange(b_packed, far)
        a_near = exchange(a_packed, near)
        a_mid = middle_part(0, a_near)
        b_mid = middle_part(1, b_far, before=a_mid[:1])
        above = shifted(first_plane, AXES, -1)
        below = shifted(carried, AXES, 1)
        b_back = exchange(b_mid, far)
        a_back = exchange(a_mid, near)
        a_home = backward_repack(0, a_back, after=[above, below])
        b_home = backward_repack(1, b_back, before=a_home[:1])
        a_done = exchange(a_home, far)
        b_done = exchange(b_home, near)
        (local,) = call(
            functools.partial(local_kernel, step),
            [whole],
            [scales, field, above, below, couplings, noise],
            scratch=[pltpu.VMEM(field.shape, noise.dtype), pltpu.SemaphoreType.DMA(())],
            specs={5: in_hbm},
            before=a_home[:1],
        )
        (sums,) = call(
            backward_kernel,
            [whole],
            [others[1][2], others[1][3]] + b_done,
            lead=waits(near, 2),
            after=[local],
        )
        edges = step == 0
        field, *planes_out = call(
            functools.partial(advance_kernel, edges),
            [whole] + [plane_shape] * 2 * edges,
            a_done
            + [others[0][2], others[0][3], out_of_depth, sums, local, field, couplings],
            lead=waits(far),
            specs={len(a_done) + 6: in_hbm},
            scratch=[pltpu.VMEM(whole.shape, jnp.float32)]
            + ([bond_held, pltpu.SemaphoreType.DMA(())] if edges else [pltpu.SemaphoreType.DMA((planes,))]),
            out_specs=None if edges else {0: in_hbm},
        )
        if edges:
            first_plane, carried = planes_out
    return (field[None], labels)


def solution(mesh):
    return jax.shard_map(
        on_device,
        mesh=mesh,
        in_specs=(
            P(("groups", "temp"), None, ("slab", "pen"), None, None),
            P("groups", ("slab", "pen"), None, None),
            P(None, ("groups", "temp"), None, ("slab", "pen"), None, None),
            P(None, None, ("slab", "pen"), None),
            P(),
            P("groups"),
            P("groups"),
        ),
        out_specs=(P(("groups", "temp"), None, ("slab", "pen"), None, None), P("groups")),
        check_vma=False,
    )
```
